32 devices in a mesh: blocks: 8 (over z, x), rep: 4 (over y, core).
Axes of the slice: x: 2, y: 2, z: 4, core: 2. Of those that a mesh axis runs over, the one named last changes fastest.
Arguments:
- features: bfloat16 [4, 32, 512, 128], P('rep', 'blocks'), may hold values from -6 to 6
- weight_one: bfloat16 [27, 128, 128], replicated, may hold values from -0.109375 to 0.109375
- weight_two: bfloat16 [27, 128, 128], replicated, may hold values from -0.109375 to 0.109375
- cotangent: bfloat16 [4, 32, 512, 128], P('rep', 'blocks'), may hold values from -6 to 6
- neighbours: int32 [4, 32, 26], P('rep', 'blocks'), may hold values from -1 to 31, as said below
Outputs:
- segment_out: bfloat16 [4, 32, 512, 128], P('rep', 'blocks')
- grad_one: float32 [27, 128, 128], replicated
- grad_two: float32 [27, 128, 128], replicated
The draws below stay inside these ranges and needn't reach their ends.
Inputs may be any that keep to these rules, and one draw needn't show every extreme that they name: neighbours[s, b, k] is the active block at offset k from block b in the slab of scene s, or -1 where that block is empty or outside the slab; blocks are ordered by x, then within each cross-section of 4 x 4 blocks by the Morton alternate of y and z, taken in reverse on odd x; block b belongs to device b // 4 of the axis blocks; the relation is symmetric (b names n at an offset exactly when n names b at the opposite one); the devices of a block and of any of its neighbours differ by at most 7 in index, and in every scene some pair differs by exactly 7.
All inputs are finite; a program needn't handle non-finite values.
Results may differ from the reference program's by a relative error of at most 0.005.
Values may be sent and summed in bfloat16 or wider, within the bound.
A program may use at most 128 MiB of HBM per device.

```python
import math
import jax
import jax.numpy as jnp
import numpy as np
from jax import lax

CH = 128
BLOCKS_DEV = 4
TOTAL_BLOCKS = 32
SCENES = 4


def offset_list_drawn():
    return [(step_x, step_y, step_z) for step_x in (-1, 0, 1) for step_y in (-1, 0, 1) for step_z in (-1, 0, 1) if (step_x, step_y, step_z) != (0, 0, 0)]


def morton_code(coord_y, coord_z):
    return coord_y % 2 + 2 * (coord_z % 2) + 4 * (coord_y // 2) + 8 * (coord_z // 2)


def morton_y(morton_val):
    return morton_val % 2 + 2 * (morton_val // 4 % 2)


def morton_z(morton_val):
    return morton_val // 2 % 2 + 2 * (morton_val // 8 % 2)


def slice_cells(perm_key, slice_count, forced):
    if forced:
        perm_part = jax.random.permutation(perm_key, 15).astype(jnp.int32)
        inverse_part = jnp.zeros((15,), jnp.int32).at[perm_part].set(jnp.arange(15, dtype=jnp.int32))
        return jnp.concatenate([(inverse_part < slice_count - 1).astype(jnp.int32), jnp.ones((1,), jnp.int32)])
    perm_all = jax.random.permutation(perm_key, 16).astype(jnp.int32)
    inverse_all = jnp.zeros((16,), jnp.int32).at[perm_all].set(jnp.arange(16, dtype=jnp.int32))
    return (inverse_all < slice_count).astype(jnp.int32)


def scene_links(scene_key):
    reach_val = (BLOCKS_DEV + 24) // BLOCKS_DEV
    lead_count = max(0, reach_val * BLOCKS_DEV - 31)
    slice_total = TOTAL_BLOCKS // 10 + 3
    span_cap = (reach_val + 1) * BLOCKS_DEV
    cell_total = 16 * slice_total
    first_order = jnp.zeros((), jnp.int32)
    last_first = jnp.zeros((), jnp.int32)
    last_count = jnp.zeros((), jnp.int32)
    by_position = []
    for slice_id in range(slice_total):
        hole_key, perm_key = jax.random.split(jax.random.fold_in(scene_key, slice_id + 1))
        wanted = (16 - jax.random.randint(hole_key, (), 0, 3)).astype(jnp.int32)
        if slice_id == 0:
            slice_count = jnp.full((), lead_count, jnp.int32)
        elif slice_id == 1:
            slice_count = jnp.full((), 16, jnp.int32)
        else:
            slice_count = jnp.minimum(wanted, span_cap - last_first % BLOCKS_DEV - last_count)
            if slice_id == 2:
                slice_count = jnp.maximum(slice_count, reach_val * BLOCKS_DEV - 15 - lead_count)
        slice_count = slice_count.astype(jnp.int32)
        occupied_m = slice_cells(perm_key, slice_count, slice_id in (1, 2))
        by_position.append(occupied_m if slice_id % 2 == 0 else occupied_m[::-1])
        last_first = first_order
        last_count = slice_count
        first_order = (first_order + slice_count).astype(jnp.int32)
    occupied = jnp.concatenate(by_position).astype(jnp.int32)
    order_pos = (jnp.cumsum(occupied) - 1).astype(jnp.int32)
    active = (occupied == 1) & (order_pos < TOTAL_BLOCKS)
    cell_codes = jnp.arange(cell_total, dtype=jnp.int32)
    block_codes = jnp.zeros((TOTAL_BLOCKS,), jnp.int32).at[jnp.where(active, order_pos, TOTAL_BLOCKS)].set(cell_codes, mode='drop')
    coord_x = block_codes // 16
    place_in = block_codes % 16
    morton_val = jnp.where(coord_x % 2 == 0, place_in, 15 - place_in)
    coord_y = morton_y(morton_val)
    coord_z = morton_z(morton_val)
    columns = []
    for offset in offset_list_drawn():
        near_x = coord_x + offset[0]
        near_y = coord_y + offset[1]
        near_z = coord_z + offset[2]
        inside = (near_x >= 0) & (near_x < slice_total) & (near_y >= 0) & (near_y <= 3) & (near_z >= 0) & (near_z <= 3)
        safe_x = jnp.clip(near_x, 0, slice_total - 1)
        safe_m = morton_code(jnp.clip(near_y, 0, 3), jnp.clip(near_z, 0, 3))
        near_code = (16 * safe_x + jnp.where(safe_x % 2 == 0, safe_m, 15 - safe_m)).astype(jnp.int32)
        inside = inside & active[near_code]
        columns.append(jnp.where(inside, order_pos[near_code], -1))
    return jnp.stack(columns, axis=1).astype(jnp.int32)


def draw_neighbours(key, part):
    scene_keys = jax.random.split(key, SCENES)
    return jax.vmap(scene_links)(scene_keys)


def steps_of(key, shape, cuts, least, top_value):
    factor_of = 1.0
    for dim, shards_of in cuts:
        draws = jax.random.uniform(jax.random.fold_in(jax.random.fold_in(key, 6), dim), (shards_of,), jnp.float32, least / len(cuts), top_value / len(cuts))
        factor_of = factor_of * jnp.repeat(jnp.exp(draws), shape[dim] // shards_of).reshape((-1,) + (1,) * (len(shape) - 1 - dim))
    return factor_of


def noise(rng, dims, width, bound, cuts=(), kind=jnp.bfloat16):
    result = width * jax.random.normal(rng, dims, jnp.float32)
    if cuts:
        result = result * steps_of(rng, dims, cuts, -0.22, 0.18)
    return jnp.clip(result, -bound, bound).astype(kind)


def setup_inputs(seed: int = 0) -> dict:
    keys = jax.random.split(jax.random.key(seed), 6)
    return {
        "features": noise(keys[0], (SCENES, TOTAL_BLOCKS, 512, CH), 1.0, 6.0, ((0, 4), (1, 8))),
        "weight_one": noise(keys[1], (27, CH, CH), (27 * CH) ** -0.5, 0.109375),
        "weight_two": noise(keys[2], (27, CH, CH), (27 * CH) ** -0.5, 0.109375),
        "cotangent": noise(keys[3], (SCENES, TOTAL_BLOCKS, 512, CH), 1.0, 6.0, ((0, 4), (1, 8))),
        "neighbours": draw_neighbours(jax.random.fold_in(keys[5], 71), 0),
    }


def offset_list():
    return [(step_x, step_y, step_z) for step_x in (-1, 0, 1) for step_y in (-1, 0, 1) for step_z in (-1, 0, 1) if (step_x, step_y, step_z) != (0, 0, 0)]

def source_range(step_val):
    if step_val == 1:
        return (0, 1)
    if step_val == -1:
        return (7, 8)
    return (0, 8)

def voxel_index(offset):
    ranges = [source_range(step_val) for step_val in offset]
    along_i = np.arange(ranges[0][0], ranges[0][1])
    along_j = np.arange(ranges[1][0], ranges[1][1])
    along_l = np.arange(ranges[2][0], ranges[2][1])
    flat_index = (along_i[:, None, None] * 64 + along_j[None, :, None] * 8 + along_l[None, None, :]).reshape(-1)
    sub_shape = (len(along_i), len(along_j), len(along_l))
    return (flat_index, sub_shape)

def build_padded(own_blocks, table, placed):
    block_count = own_blocks.shape[0]
    channels = own_blocks.shape[2]
    pieces = {(0, 0, 0): own_blocks.reshape(block_count, 8, 8, 8, channels)}
    for k_index, offset in enumerate(offset_list()):
        flat_index, sub_shape = voxel_index(offset)
        picked = jnp.take(table, jnp.asarray(flat_index, dtype=jnp.int32), axis=1)
        column = placed[:, k_index]
        got_rows = jnp.take(picked, jnp.maximum(column, 0).astype(jnp.int32), axis=0)
        got_rows = jnp.where((column >= 0)[:, None, None], got_rows, jnp.zeros_like(got_rows))
        pieces[offset] = got_rows.reshape((block_count,) + sub_shape + (channels,))
    planes = []
    for step_x in (-1, 0, 1):
        lines = []
        for step_y in (-1, 0, 1):
            lines.append(jnp.concatenate([pieces[step_x, step_y, step_z] for step_z in (-1, 0, 1)], axis=3))
        planes.append(jnp.concatenate(lines, axis=2))
    return jnp.concatenate(planes, axis=1)

def tap_slab(padded, tap_a):
    block_count = padded.shape[0]
    channels = padded.shape[-1]
    return jnp.concatenate([padded[:, tap_a:tap_a + 8, tap_b:tap_b + 8, tap_c:tap_c + 8, :].reshape(block_count * 512, channels) for tap_b in range(3) for tap_c in range(3)], axis=1)

def conv_taps(padded, weights):
    block_count = padded.shape[0]
    channels = padded.shape[-1]
    summed = jnp.zeros((block_count * 512, weights.shape[2]), jnp.float32)
    for tap_a in range(3):
        kernel = weights[9 * tap_a:9 * tap_a + 9].reshape(9 * channels, weights.shape[2])
        summed = summed + jnp.dot(tap_slab(padded, tap_a), kernel, preferred_element_type=jnp.float32)
    return summed

def weight_taps(padded, grad_rows):
    channels = padded.shape[-1]
    width_out = grad_rows.shape[1]
    parts_list = []
    for tap_a in range(3):
        product = lax.dot_general(tap_slab(padded, tap_a), grad_rows, (((0,), (0,)), ((), ())), preferred_element_type=jnp.float32)
        parts_list.append(product.reshape(9, channels, width_out))
    return jnp.concatenate(parts_list, axis=0)

def silu_slope(values):
    sigmoid_val = jax.nn.sigmoid(values)
    return sigmoid_val * (1.0 + values * (1.0 - sigmoid_val))

def reference(features, weight_one, weight_two, cotangent, neighbours):
    flipped = jnp.transpose(weight_two[::-1], (0, 2, 1))
    grad_one = jnp.zeros((27, CH, CH), jnp.float32)
    grad_two = jnp.zeros((27, CH, CH), jnp.float32)
    outputs = []
    for scene_index in range(SCENES):
        blocks = features[scene_index]
        cot_blocks = cotangent[scene_index]
        link_table = neighbours[scene_index]
        input_pad = build_padded(blocks, blocks, link_table)
        pre_act = conv_taps(input_pad, weight_one)
        hidden = jax.nn.silu(pre_act).astype(jnp.bfloat16)
        hidden_blocks = hidden.reshape(TOTAL_BLOCKS, 512, CH)
        hidden_pad = build_padded(hidden_blocks, hidden_blocks, link_table)
        outputs.append(conv_taps(hidden_pad, weight_two).astype(jnp.bfloat16).reshape(TOTAL_BLOCKS, 512, CH))
        grad_two = grad_two + weight_taps(hidden_pad, cot_blocks.reshape(-1, CH))
        cot_pad = build_padded(cot_blocks, cot_blocks, link_table)
        back_rows = conv_taps(cot_pad, flipped)
        delta_rows = (back_rows * silu_slope(pre_act)).astype(jnp.bfloat16)
        grad_one = grad_one + weight_taps(input_pad, delta_rows)
    norm_scale = 1.0 / math.sqrt(SCENES * TOTAL_BLOCKS * 512)
    return (jnp.stack(outputs), grad_one * norm_scale, grad_two * norm_scale)
```

```python
import functools
import math

import jax
import jax.numpy as jnp
from jax import lax
from jax.experimental import pallas as pl
from jax.experimental.pallas import tpu as pltpu
from jax.sharding import PartitionSpec as P

VMEM_LIMIT = 56 * 1024 * 1024


def offset_index(step_x, step_y, step_z):
    place = 9 * (step_x + 1) + 3 * (step_y + 1) + (step_z + 1)
    return place if place < 13 else place - 1


def from_behind(block, axis, distance):
    devices = range(lax.axis_size(axis))
    route = [(i - distance, i) for i in devices if i - distance in devices]
    return lax.ppermute(block, axis, route)


def lines_of(rows):
    return rows.astype(jnp.float32).reshape(-1, 8, rows.shape[-1])


def build_slab(block, own_ref, table_ref, place_ref, pad_ref, slab_ref):
    channels = own_ref.shape[-1]

    def place(step_x, step_y, step_z):
        return place_ref[block, offset_index(step_x, step_y, step_z)]

    def source(step_x, step_y, step_z, plane, rows):
        if (step_x, step_y, step_z) == (0, 0, 0):
            return lines_of(own_ref[block, plane, rows, :])
        where = place(step_x, step_y, step_z)
        got = lines_of(table_ref[jnp.maximum(where, 0), plane, rows, :])
        return jnp.where(where >= 0, got, 0.0)

    def put(ii, first_line, step_x, step_y, plane, rows, pick):
        mid, low, high = (
            source(step_x, step_y, step_z, plane, rows)[pick] for step_z in (0, -1, 1)
        )
        cell = lax.broadcasted_iota(jnp.int32, mid.shape, 1)
        count = mid.shape[0]
        shifted = (
            pltpu.roll(jnp.where(cell == 7, low, mid), 1, 1),
            mid,
            pltpu.roll(jnp.where(cell == 0, high, mid), 7, 1),
        )
        for tap_c in range(3):
            pad_ref[tap_c, ii, pl.ds(8 * first_line, 8 * count), :] = shifted[tap_c].reshape(
                8 * count, channels
            )

    every = slice(None)
    for ii in range(10):
        step_x = -1 if ii == 0 else (1 if ii == 9 else 0)
        plane = 7 if ii == 0 else (0 if ii == 9 else ii - 1)
        put(ii, 0, step_x, -1, plane, slice(48, 64), slice(1, 2))
        put(ii, 1, step_x, 0, plane, slice(0, 64), every)
        put(ii, 9, step_x, 1, plane, slice(0, 16), slice(0, 1))
    for tap_b in range(3):
        for tap_c in range(3):
            column = (3 * tap_b + tap_c) * channels
            slab_ref[:, pl.ds(column, channels)] = (
                pad_ref[tap_c, :, pl.ds(8 * tap_b, 64), :]
                .reshape(640, channels)
                .astype(jnp.bfloat16)
            )


def conv_slab(slab_ref, weight_ref):
    total = None
    for tap_a in range(3):
        part = jnp.dot(
            slab_ref[pl.ds(64 * tap_a, 512), :],
            weight_ref[tap_a],
            preferred_element_type=jnp.float32,
        )
        total = part if total is None else total + part
    return total


def spread_rows(spread_ref, rows):
    channels = rows.shape[-1]
    spread_ref[...] = jnp.zeros_like(spread_ref)
    for tap_a in range(3):
        spread_ref[pl.ds(64 * tap_a, 512), pl.ds(tap_a * channels, channels)] = rows


def add_taps(total_ref, spread_ref, slab_ref):
    total_ref[...] += jnp.dot(
        spread_ref[...].T, slab_ref[...], preferred_element_type=jnp.float32
    )


def write_taps(total_ref, grad_ref, scale):
    channels = grad_ref.shape[-1]
    for tap_a in range(3):
        for tap_bc in range(9):
            piece = total_ref[
                pl.ds(tap_a * channels, channels), pl.ds(tap_bc * channels, channels)
            ]
            grad_ref[9 * tap_a + tap_bc] = piece.T * scale


def sigmoid(values):
    return 1.0 / (1.0 + jnp.exp(-values))


def first_kernel(place_ref, own_ref, table_ref, weight_ref, pre_ref, hidden_ref, pad_ref, slab_ref):
    def step(block, carry):
        build_slab(block, own_ref, table_ref, place_ref, pad_ref, slab_ref)
        pre = conv_slab(slab_ref, weight_ref)
        pre_ref[block] = pre
        hidden_ref[block] = (pre / (1.0 + jnp.exp(-pre))).astype(jnp.bfloat16)
        return carry

    lax.fori_loop(0, own_ref.shape[0], step, 0)


def back_kernel(
    scale, place_ref, own_ref, table_ref, cot_ref, cot_table_ref, weight_ref, pre_ref,
    grad_ref, pad_ref, slab_ref, spread_ref, total_ref,
):
    total_ref[...] = jnp.zeros_like(total_ref)

    def step(block, carry):
        build_slab(block, cot_ref, cot_table_ref, place_ref, pad_ref, slab_ref)
        back = conv_slab(slab_ref, weight_ref)
        pre = pre_ref[block]
        sig = sigmoid(pre)
        delta = (back * (sig * (1.0 + pre * (1.0 - sig)))).astype(jnp.bfloat16)
        spread_rows(spread_ref, delta)
        build_slab(block, own_ref, table_ref, place_ref, pad_ref, slab_ref)
        add_taps(total_ref, spread_ref, slab_ref)
        return carry

    lax.fori_loop(0, own_ref.shape[0], step, 0)
    write_taps(total_ref, grad_ref, scale)


def second_kernel(
    scale, place_ref, own_ref, table_ref, cot_ref, weight_ref,
    out_ref, grad_ref, pad_ref, slab_ref, spread_ref, total_ref,
):
    total_ref[...] = jnp.zeros_like(total_ref)

    def step(block, carry):
        build_slab(block, own_ref, table_ref, place_ref, pad_ref, slab_ref)
        out_ref[block] = conv_slab(slab_ref, weight_ref).astype(jnp.bfloat16)
        spread_rows(spread_ref, cot_ref[block].reshape(512, cot_ref.shape[-1]))
        add_taps(total_ref, spread_ref, slab_ref)
        return carry

    lax.fori_loop(0, own_ref.shape[0], step, 0)
    write_taps(total_ref, grad_ref, scale)


def call(body, outs, scratch, flops, *operands):
    space = pl.BlockSpec(memory_space=pltpu.VMEM)
    specs = [pl.BlockSpec(memory_space=pltpu.SMEM)] + [space] * (len(operands) - 1)
    moved = sum(x.size * x.dtype.itemsize for x in operands)
    return pl.pallas_call(
        body,
        out_shape=outs,
        in_specs=specs,
        out_specs=[space] * len(outs),
        scratch_shapes=scratch,
        compiler_params=pltpu.CompilerParams(vmem_limit_bytes=VMEM_LIMIT),
        cost_estimate=pl.CostEstimate(flops=flops, bytes_accessed=moved, transcendentals=0),
    )(*operands)


def local(features, weight_one, weight_two, cotangent, neighbours):
    block_count, channels = features.shape[1], features.shape[3]
    devices = lax.axis_size("blocks")
    reach = (block_count + 24) // block_count
    own = features[0].reshape(block_count, 8, 64, channels)
    cot = cotangent[0].reshape(block_count, 8, 64, channels)
    links = neighbours[0]
    whole = devices <= 2 * reach + 1
    if whole:
        placed = links
    else:
        gap = links // block_count - lax.axis_index("blocks")
        placed = jnp.where(links >= 0, (gap + reach) * block_count + links % block_count, -1)

    def collect(payload):
        if whole:
            return lax.all_gather(payload, "blocks", axis=0, tiled=True)
        pieces = [
            payload if gap == 0 else from_behind(payload, "blocks", -gap)
            for gap in range(-reach, reach + 1)
        ]
        return jnp.concatenate(pieces, axis=0)

    def slabs(weights):
        return weights.reshape(3, 9 * channels, channels)

    flipped = jnp.transpose(weight_two[::-1], (0, 2, 1))
    voxels = lax.axis_size("rep") * devices * block_count * 512
    scale = 1.0 / math.sqrt(voxels)
    flops = 2 * block_count * 512 * 27 * channels * channels
    f32, bf16 = jnp.float32, jnp.bfloat16
    pad = pltpu.VMEM((3, 10, 80, channels), f32)
    slab = pltpu.VMEM((640, 9 * channels), bf16)
    spread = pltpu.VMEM((640, 3 * channels), bf16)
    total = pltpu.VMEM((3 * channels, 9 * channels), f32)
    rows = (block_count, 512, channels)
    grads = jax.ShapeDtypeStruct(weight_one.shape, f32)

    table = collect(own)
    cot_table = collect(cot)
    pre, hidden = call(
        first_kernel,
        [jax.ShapeDtypeStruct(rows, f32), jax.ShapeDtypeStruct(rows, bf16)],
        [pad, slab], flops,
        placed, own, table, slabs(weight_one),
    )
    hidden = hidden.reshape(own.shape)
    hidden_table = collect(hidden)
    (grad_one,) = call(
        functools.partial(back_kernel, scale),
        [grads], [pad, slab, spread, total], 2 * flops,
        placed, own, table, cot, cot_table, slabs(flipped), pre,
    )
    grad_one = lax.psum(grad_one, ("blocks", "rep"))
    out, grad_two = call(
        functools.partial(second_kernel, scale),
        [jax.ShapeDtypeStruct(rows, bf16), grads], [pad, slab, spread, total], 2 * flops,
        placed, hidden, hidden_table, cot, slabs(weight_two),
    )
    grad_two = lax.psum(grad_two, ("blocks", "rep"))
    return out.reshape(features.shape), grad_one, grad_two


def solution(mesh):
    in_specs = (
        P("rep", "blocks", None, None),
        P(),
        P(),
        P("rep", "blocks", None, None),
        P("rep", "blocks", None),
    )
    out_specs = (P("rep", "blocks", None, None), P(), P())
    return jax.shard_map(local, mesh=mesh, in_specs=in_specs, out_specs=out_specs, check_vma=False)
```

```python
import functools
import math

import jax
import jax.numpy as jnp
from jax import lax
from jax.experimental import pallas as pl
from jax.experimental.pallas import tpu as pltpu
from jax.sharding import PartitionSpec as P

VMEM_LIMIT = 56 * 1024 * 1024


def offset_index(step_x, step_y, step_z):
    place = 9 * (step_x + 1) + 3 * (step_y + 1) + (step_z + 1)
    return place if place < 13 else place - 1


def from_behind(block, axis, distance):
    devices = range(lax.axis_size(axis))
    route = [(i - distance, i) for i in devices if i - distance in devices]
    return lax.ppermute(block, axis, route)


def lines_of(rows):
    return rows.astype(jnp.float32).reshape(-1, 8, rows.shape[-1])


def plane_start(plane):
    return {0: 0, 7: 64}.get(plane, 128 + 32 * (plane - 1))


def pack_shell(block, own_ref, shell_ref):
    channels = own_ref.shape[-1]
    for plane in (0, 7):
        shell_ref[block, pl.ds(plane_start(plane), 64), :] = own_ref[block, plane]
    for plane in range(1, 7):
        lines = lines_of(own_ref[block, plane])
        cell = lax.broadcasted_iota(jnp.int32, (1, 8, channels), 1)
        ends = []
        for group in (0, 4):
            packed = pltpu.roll(lines[group : group + 1], 1, 1)
            for turn in range(1, 4):
                line = pltpu.roll(lines[group + turn : group + turn + 1], 2 * turn + 1, 1)
                packed = jnp.where(cell >= 2 * turn, line, packed)
            ends.append(packed)
        packed = jnp.concatenate([lines[0:1], lines[7:8]] + ends, axis=0)
        shell_ref[block, pl.ds(plane_start(plane), 32), :] = packed.reshape(32, channels).astype(
            jnp.bfloat16
        )


def build_slab(block, own_ref, table_ref, place_ref, pad_ref, slab_ref):
    channels = own_ref.shape[-1]

    def source(step_x, step_y, step_z, plane):
        if (step_x, step_y, step_z) == (0, 0, 0):
            return lines_of(own_ref[block, plane])
        where = place_ref[block, offset_index(step_x, step_y, step_z)]
        near, start = jnp.maximum(where, 0), plane_start(plane)
        if plane in (0, 7):
            if step_y == 0:
                got = lines_of(table_ref[near, pl.ds(start, 64), :])
            elif step_y == 1:
                got = lines_of(table_ref[near, pl.ds(start, 16), :])[0:1]
            else:
                got = lines_of(table_ref[near, pl.ds(start + 48, 16), :])[1:2]
        elif step_y == 0:
            ends = lines_of(table_ref[near, pl.ds(start + 16, 16), :])
            got = jnp.concatenate(
                [
                    pltpu.roll(ends[j // 4 : j // 4 + 1], 7 - 2 * (j % 4), 1)
                    for j in range(8)
                ],
                axis=0,
            )
        else:
            got = lines_of(table_ref[near, pl.ds(start, 16), :])
            got = got[0:1] if step_y == 1 else got[1:2]
        return jnp.where(where >= 0, got, 0.0)

    def put(ii, first_line, step_x, step_y, plane):
        mid, low, high = (source(step_x, step_y, step_z, plane) for step_z in (0, -1, 1))
        cell = lax.broadcasted_iota(jnp.int32, mid.shape, 1)
        count = mid.shape[0]
        shifted = (
            pltpu.roll(jnp.where(cell == 7, low, mid), 1, 1),
            mid,
            pltpu.roll(jnp.where(cell == 0, high, mid), 7, 1),
        )
        for tap_c in range(3):
            pad_ref[tap_c, ii, pl.ds(8 * first_line, 8 * count), :] = shifted[tap_c].reshape(
                8 * count, channels
            )

    for ii in range(10):
        step_x = -1 if ii == 0 else (1 if ii == 9 else 0)
        plane = 7 if ii == 0 else (0 if ii == 9 else ii - 1)
        put(ii, 0, step_x, -1, plane)
        put(ii, 1, step_x, 0, plane)
        put(ii, 9, step_x, 1, plane)
    for tap_b in range(3):
        for tap_c in range(3):
            column = (3 * tap_b + tap_c) * channels
            slab_ref[:, pl.ds(column, channels)] = (
                pad_ref[tap_c, :, pl.ds(8 * tap_b, 64), :]
                .reshape(640, channels)
                .astype(jnp.bfloat16)
            )


def conv_slab(slab_ref, weight_ref):
    total = None
    for tap_a in range(3):
        part = jnp.dot(
            slab_ref[pl.ds(64 * tap_a, 512), :],
            weight_ref[tap_a],
            preferred_element_type=jnp.float32,
        )
        total = part if total is None else total + part
    return total


def spread_rows(spread_ref, rows):
    channels = rows.shape[-1]
    spread_ref[...] = jnp.zeros_like(spread_ref)
    for tap_a in range(3):
        spread_ref[pl.ds(64 * tap_a, 512), pl.ds(tap_a * channels, channels)] = rows


def add_taps(total_ref, spread_ref, slab_ref):
    total_ref[...] += jnp.dot(
        spread_ref[...].T, slab_ref[...], preferred_element_type=jnp.float32
    )


def write_taps(total_ref, grad_ref, scale):
    channels = grad_ref.shape[-1]
    for tap_a in range(3):
        for tap_bc in range(9):
            piece = total_ref[
                pl.ds(tap_a * channels, channels), pl.ds(tap_bc * channels, channels)
            ]
            grad_ref[9 * tap_a + tap_bc] = piece.T * scale


def sigmoid(values):
    return 1.0 / (1.0 + jnp.exp(-values))


def pack_kernel(own_ref, cot_ref, own_shell_ref, cot_shell_ref):
    def step(block, carry):
        pack_shell(block, own_ref, own_shell_ref)
        pack_shell(block, cot_ref, cot_shell_ref)
        return carry

    lax.fori_loop(0, own_ref.shape[0], step, 0)


def first_kernel(
    place_ref, own_ref, table_ref, weight_ref, pre_ref, hidden_ref, shell_ref, pad_ref, slab_ref
):
    def step(block, carry):
        build_slab(block, own_ref, table_ref, place_ref, pad_ref, slab_ref)
        pre = conv_slab(slab_ref, weight_ref)
        pre_ref[block] = pre
        hidden = (pre / (1.0 + jnp.exp(-pre))).astype(jnp.bfloat16)
        hidden_ref[block] = hidden.reshape(hidden_ref.shape[1:])
        pack_shell(block, hidden_ref, shell_ref)
        return carry

    lax.fori_loop(0, own_ref.shape[0], step, 0)


def back_kernel(
    scale, place_ref, own_ref, table_ref, cot_ref, cot_table_ref, weight_ref, pre_ref,
    grad_ref, pad_ref, slab_ref, spread_ref, total_ref,
):
    total_ref[...] = jnp.zeros_like(total_ref)

    def step(block, carry):
        build_slab(block, cot_ref, cot_table_ref, place_ref, pad_ref, slab_ref)
        back = conv_slab(slab_ref, weight_ref)
        pre = pre_ref[block]
        sig = sigmoid(pre)
        delta = (back * (sig * (1.0 + pre * (1.0 - sig)))).astype(jnp.bfloat16)
        spread_rows(spread_ref, delta)
        build_slab(block, own_ref, table_ref, place_ref, pad_ref, slab_ref)
        add_taps(total_ref, spread_ref, slab_ref)
        return carry

    lax.fori_loop(0, own_ref.shape[0], step, 0)
    write_taps(total_ref, grad_ref, scale)


def second_kernel(
    scale, place_ref, own_ref, table_ref, cot_ref, weight_ref,
    out_ref, grad_ref, pad_ref, slab_ref, spread_ref, total_ref,
):
    total_ref[...] = jnp.zeros_like(total_ref)

    def step(block, carry):
        build_slab(block, own_ref, table_ref, place_ref, pad_ref, slab_ref)
        out_ref[block] = conv_slab(slab_ref, weight_ref).astype(jnp.bfloat16)
        spread_rows(spread_ref, cot_ref[block].reshape(512, cot_ref.shape[-1]))
        add_taps(total_ref, spread_ref, slab_ref)
        return carry

    lax.fori_loop(0, own_ref.shape[0], step, 0)
    write_taps(total_ref, grad_ref, scale)


def ring_kernel(devices, payload_ref, table_ref, send_sem, recv_sem, own_sem):
    count = payload_ref.shape[0]
    half = count // 2
    me = lax.axis_index("blocks")
    odd = me % 2
    pos = (1 - odd) * (me // 2) + odd * (devices - 1 - me // 2)

    def index_of(position):
        spot = (position + 2 * devices) % devices
        back = spot // (devices // 2)
        return (1 - back) * 2 * spot + back * (2 * (devices - 1 - spot) + 1)

    ends = (index_of(pos + 1), index_of(pos - 1))
    barrier = pltpu.get_barrier_semaphore()
    for end in ends:
        pl.semaphore_signal(
            barrier, inc=1, device_id={"blocks": end}, device_id_type=pl.DeviceIdType.MESH
        )
    pl.semaphore_wait(barrier, 2)
    own = pltpu.make_async_copy(payload_ref, table_ref.at[pl.ds(me * count, count)], own_sem)
    own.start()
    copies = []
    for step in range(devices - 1):
        for way, sign in ((0, 1), (1, -1)):
            if step:
                copies[2 * (step - 1) + way].wait_recv()
            owner = index_of(pos - sign * step)
            target = table_ref.at[pl.ds(owner * count + way * half, half)]
            source = payload_ref.at[pl.ds(way * half, half)] if step == 0 else target
            copy = pltpu.make_async_remote_copy(
                src_ref=source,
                dst_ref=target,
                send_sem=send_sem.at[way, step],
                recv_sem=recv_sem.at[way, step],
                device_id={"blocks": ends[way]},
                device_id_type=pl.DeviceIdType.MESH,
            )
            copy.start()
            copies.append(copy)
    for copy in copies[-2:]:
        copy.wait_recv()
    for copy in copies:
        copy.wait_send()
    own.wait()


def ring_gather(payload, devices, collective_id):
    space = pl.BlockSpec(memory_space=pltpu.VMEM)
    sems = pltpu.SemaphoreType.DMA((2, devices - 1))
    return pl.pallas_call(
        functools.partial(ring_kernel, devices),
        out_shape=jax.ShapeDtypeStruct(
            (devices * payload.shape[0],) + payload.shape[1:], payload.dtype
        ),
        in_specs=[space],
        out_specs=space,
        scratch_shapes=[sems, sems, pltpu.SemaphoreType.DMA],
        compiler_params=pltpu.CompilerParams(
            collective_id=collective_id, has_side_effects=True, vmem_limit_bytes=VMEM_LIMIT
        ),
    )(payload)


def bit_orders(block_bits, rep_bits):
    first = [("rep", 0)]
    rest = [("rep", k) for k in range(1, rep_bits)]
    low = [("blocks", k) for k in range(block_bits - 1)]
    last = [("blocks", block_bits - 1)]
    turning = rest + low
    turns = [turning[t % len(turning) :] + turning[: t % len(turning)] for t in range(3)]
    return [first + turn + last for turn in turns]


def sum_kernel(orders, one_ref, two_ref, out_ref, held_ref, land_ref, send_sem, recv_sem):
    rows = out_ref.shape[0]
    share = rows // len(orders)
    levels = len(orders[0])
    place = {axis: lax.axis_index(axis) for axis in ("blocks", "rep")}

    def bit_of(dim):
        axis, k = dim
        return place[axis] // 2**k % 2

    def partner(dim):
        axis, k = dim
        return {axis: place[axis] + (1 - 2 * bit_of(dim)) * 2**k}

    barrier = pltpu.get_barrier_semaphore()
    for dim in orders[0]:
        pl.semaphore_signal(
            barrier, inc=1, device_id=partner(dim), device_id_type=pl.DeviceIdType.MESH
        )
    pl.semaphore_wait(barrier, levels)
    held_ref[pl.ds(0, rows // 2), :] = one_ref[...]
    held_ref[pl.ds(rows // 2, rows // 2), :] = two_ref[...]

    def copy_to(part, step, dim, source, target):
        return pltpu.make_async_remote_copy(
            src_ref=source,
            dst_ref=target,
            send_sem=send_sem.at[part, step],
            recv_sem=recv_sem.at[part, step],
            device_id=partner(dim),
            device_id_type=pl.DeviceIdType.MESH,
        )

    starts = [[part * share] for part in range(len(orders))]
    flying = [None] * len(orders)
    sent = []
    for step in range(levels + 1):
        half = share >> (step + 1)
        for part, order in enumerate(orders):
            if step:
                flying[part].wait_recv()
                size = share >> step
                mine = pl.ds(pl.multiple_of(starts[part][-1], 8), size)
                landed = pl.ds(part * share + share - 2 * size, size)
                summed = held_ref[mine, :] + land_ref[landed, :]
                kept_ref = held_ref if step < levels else out_ref
                kept_ref[mine, :] = summed
            if step < levels:
                bit = bit_of(order[step])
                start = starts[part][-1]
                away = pl.multiple_of(start + (1 - bit) * half, 8)
                copy = copy_to(
                    part, step, order[step],
                    held_ref.at[pl.ds(away, half)],
                    land_ref.at[pl.ds(part * share + share - 2 * half, half)],
                )
                copy.start()
                flying[part] = copy
                sent.append(copy)
                starts[part].append(start + bit * half)
    for step in reversed(range(levels)):
        size = share >> (step + 1)
        for part, order in enumerate(orders):
            if step < levels - 1:
                flying[part].wait_recv()
            mine = out_ref.at[pl.ds(pl.multiple_of(starts[part][step + 1], 8), size)]
            copy = copy_to(part, levels + step, order[step], mine, mine)
            copy.start()
            flying[part] = copy
            sent.append(copy)
    for copy in flying:
        copy.wait_recv()
    for copy in sent:
        copy.wait_send()


def sum_everywhere(one, two, block_devices, rep_devices, collective_id):
    block_bits, rep_bits = block_devices.bit_length() - 1, rep_devices.bit_length() - 1
    orders = bit_orders(block_bits, rep_bits)
    channels = one.shape[-1]
    rows = 2 * one.size // channels
    space = pl.BlockSpec(memory_space=pltpu.VMEM)
    sems = pltpu.SemaphoreType.DMA((len(orders), 2 * len(orders[0])))
    out = pl.pallas_call(
        functools.partial(sum_kernel, orders),
        out_shape=jax.ShapeDtypeStruct((rows, channels), one.dtype),
        in_specs=[space, space],
        out_specs=space,
        scratch_shapes=[pltpu.VMEM((rows, channels), one.dtype)] * 2 + [sems, sems],
        compiler_params=pltpu.CompilerParams(
            collective_id=collective_id, has_side_effects=True, vmem_limit_bytes=VMEM_LIMIT
        ),
    )(one.reshape(-1, channels), two.reshape(-1, channels))
    return out[: rows // 2].reshape(one.shape), out[rows // 2 :].reshape(two.shape)


def can_halve(count, rows):
    block_devices, rep_devices = count
    total = block_devices * rep_devices
    powers = total & (total - 1) == 0 and block_devices >= 2 and rep_devices >= 2
    return powers and rows % (3 * 8 * total) == 0


def call(body, outs, scratch, flops, *operands):
    space = pl.BlockSpec(memory_space=pltpu.VMEM)
    scalars = pl.BlockSpec(memory_space=pltpu.SMEM)
    specs = [scalars if x.dtype == jnp.int32 else space for x in operands]
    moved = sum(x.size * x.dtype.itemsize for x in operands)
    return pl.pallas_call(
        body,
        out_shape=outs,
        in_specs=specs,
        out_specs=[space] * len(outs),
        scratch_shapes=scratch,
        compiler_params=pltpu.CompilerParams(vmem_limit_bytes=VMEM_LIMIT),
        cost_estimate=pl.CostEstimate(flops=flops, bytes_accessed=moved, transcendentals=0),
    )(*operands)


def local(features, weight_one, weight_two, cotangent, neighbours):
    block_count, channels = features.shape[1], features.shape[3]
    devices = lax.axis_size("blocks")
    reach = (block_count + 24) // block_count
    own = features[0].reshape(block_count, 8, 64, channels)
    cot = cotangent[0].reshape(block_count, 8, 64, channels)
    links = neighbours[0]
    whole = devices <= 2 * reach + 1
    if whole:
        placed = links
    else:
        gap = links // block_count - lax.axis_index("blocks")
        placed = jnp.where(links >= 0, (gap + reach) * block_count + links % block_count, -1)

    ring = whole and devices % 2 == 0 and block_count % 2 == 0

    def collect(payload, collective_id=None):
        if ring and collective_id is not None:
            return ring_gather(payload, devices, collective_id)
        if whole:
            return lax.all_gather(payload, "blocks", axis=0, tiled=True)
        pieces = [
            payload if gap == 0 else from_behind(payload, "blocks", -gap)
            for gap in range(-reach, reach + 1)
        ]
        return jnp.concatenate(pieces, axis=0)

    def slabs(weights):
        return weights.reshape(3, 9 * channels, channels)

    flipped = jnp.transpose(weight_two[::-1], (0, 2, 1))
    voxels = lax.axis_size("rep") * devices * block_count * 512
    scale = 1.0 / math.sqrt(voxels)
    flops = 2 * block_count * 512 * 27 * channels * channels
    f32, bf16 = jnp.float32, jnp.bfloat16
    pad = pltpu.VMEM((3, 10, 80, channels), f32)
    slab = pltpu.VMEM((640, 9 * channels), bf16)
    spread = pltpu.VMEM((640, 3 * channels), bf16)
    total = pltpu.VMEM((3 * channels, 9 * channels), f32)
    rows = (block_count, 512, channels)
    grads = jax.ShapeDtypeStruct(weight_one.shape, f32)

    shell = jax.ShapeDtypeStruct((block_count, 320, channels), bf16)

    own_shell, cot_shell = call(pack_kernel, [shell, shell], [], 0, own, cot)
    cot_table = collect(cot_shell)
    table = collect(own_shell, 1)
    pre, hidden, hidden_shell = call(
        first_kernel,
        [jax.ShapeDtypeStruct(rows, f32), jax.ShapeDtypeStruct(own.shape, bf16), shell],
        [pad, slab], flops,
        placed, own, table, slabs(weight_one),
    )
    hidden_table = collect(hidden_shell, 2)
    out, grad_two = call(
        functools.partial(second_kernel, scale),
        [jax.ShapeDtypeStruct(rows, bf16), grads], [pad, slab, spread, total], 2 * flops,
        placed, hidden, hidden_table, cot, slabs(weight_two),
    )
    cot_table, grad_two = lax.optimization_barrier((cot_table, grad_two))
    (grad_one,) = call(
        functools.partial(back_kernel, scale),
        [grads], [pad, slab, spread, total], 2 * flops,
        placed, own, table, cot, cot_table, slabs(flipped), pre,
    )
    counts = (devices, lax.axis_size("rep"))
    if can_halve(counts, 2 * grad_one.size // channels):
        grad_one, grad_two = sum_everywhere(grad_one, grad_two, *counts, 3)
    else:
        grad_one, grad_two = lax.psum((grad_one, grad_two), ("blocks", "rep"))
    return out.reshape(features.shape), grad_one, grad_two


def solution(mesh):
    in_specs = (
        P("rep", "blocks", None, None),
        P(),
        P(),
        P("rep", "blocks", None, None),
        P("rep", "blocks", None),
    )
    out_specs = (P("rep", "blocks", None, None), P(), P())
    return jax.shard_map(local, mesh=mesh, in_specs=in_specs, out_specs=out_specs, check_vma=False)
```

```python
import functools
import math

import jax
import jax.numpy as jnp
from jax import lax
from jax.experimental import pallas as pl
from jax.experimental.pallas import tpu as pltpu
from jax.sharding import PartitionSpec as P

VMEM_LIMIT = 56 * 1024 * 1024
SHELL = 320
CUTS = 2


def offset_index(step_x, step_y, step_z):
    place = 9 * (step_x + 1) + 3 * (step_y + 1) + (step_z + 1)
    return place if place < 13 else place - 1


def from_behind(block, axis, distance):
    devices = range(lax.axis_size(axis))
    route = [(i - distance, i) for i in devices if i - distance in devices]
    return lax.ppermute(block, axis, route)


def lines_of(rows):
    return rows.astype(jnp.float32).reshape(-1, 8, rows.shape[-1])


def plane_start(plane):
    return {0: 0, 7: 64}.get(plane, 128 + 32 * (plane - 1))


def pack_shell(block, own_ref, shell_ref, base=0):
    channels = own_ref.shape[-1]
    for plane in (0, 7):
        shell_ref[block, pl.ds(base + plane_start(plane), 64), :] = own_ref[block, plane]
    for plane in range(1, 7):
        lines = lines_of(own_ref[block, plane])
        cell = lax.broadcasted_iota(jnp.int32, (1, 8, channels), 1)
        ends = []
        for group in (0, 4):
            packed = pltpu.roll(lines[group : group + 1], 1, 1)
            for turn in range(1, 4):
                line = pltpu.roll(lines[group + turn : group + turn + 1], 2 * turn + 1, 1)
                packed = jnp.where(cell >= 2 * turn, line, packed)
            ends.append(packed)
        packed = jnp.concatenate([lines[0:1], lines[7:8]] + ends, axis=0)
        packed = packed.reshape(32, channels).astype(jnp.bfloat16)
        shell_ref[block, pl.ds(base + plane_start(plane), 32), :] = packed


def build_slab(block, own_ref, table_ref, place_ref, pad_ref, slab_ref, base=0):
    channels = own_ref.shape[-1]

    def source(step_x, step_y, step_z, plane):
        if (step_x, step_y, step_z) == (0, 0, 0):
            return lines_of(own_ref[block, plane])
        where = place_ref[block, offset_index(step_x, step_y, step_z)]
        near, start = jnp.maximum(where, 0), base + plane_start(plane)
        if plane in (0, 7):
            if step_y == 0:
                got = lines_of(table_ref[near, pl.ds(start, 64), :])
            elif step_y == 1:
                got = lines_of(table_ref[near, pl.ds(start, 16), :])[0:1]
            else:
                got = lines_of(table_ref[near, pl.ds(start + 48, 16), :])[1:2]
        elif step_y == 0:
            ends = lines_of(table_ref[near, pl.ds(start + 16, 16), :])
            got = jnp.concatenate(
                [
                    pltpu.roll(ends[j // 4 : j // 4 + 1], 7 - 2 * (j % 4), 1)
                    for j in range(8)
                ],
                axis=0,
            )
        else:
            got = lines_of(table_ref[near, pl.ds(start, 16), :])
            got = got[0:1] if step_y == 1 else got[1:2]
        return jnp.where(where >= 0, got, 0.0)

    def put(ii, first_line, step_x, step_y, plane):
        mid, low, high = (source(step_x, step_y, step_z, plane) for step_z in (0, -1, 1))
        cell = lax.broadcasted_iota(jnp.int32, mid.shape, 1)
        count = mid.shape[0]
        shifted = (
            pltpu.roll(jnp.where(cell == 7, low, mid), 1, 1),
            mid,
            pltpu.roll(jnp.where(cell == 0, high, mid), 7, 1),
        )
        for tap_c in range(3):
            pad_ref[tap_c, ii, pl.ds(8 * first_line, 8 * count), :] = shifted[tap_c].reshape(
                8 * count, channels
            )

    for ii in range(10):
        step_x = -1 if ii == 0 else (1 if ii == 9 else 0)
        plane = 7 if ii == 0 else (0 if ii == 9 else ii - 1)
        put(ii, 0, step_x, -1, plane)
        put(ii, 1, step_x, 0, plane)
        put(ii, 9, step_x, 1, plane)
    for tap_b in range(3):
        for tap_c in range(3):
            column = (3 * tap_b + tap_c) * channels
            slab_ref[:, pl.ds(column, channels)] = (
                pad_ref[tap_c, :, pl.ds(8 * tap_b, 64), :]
                .reshape(640, channels)
                .astype(jnp.bfloat16)
            )


def conv_slab(slab_ref, weight_ref):
    total = None
    for tap_a in range(3):
        part = jnp.dot(
            slab_ref[pl.ds(64 * tap_a, 512), :],
            weight_ref[tap_a],
            preferred_element_type=jnp.float32,
        )
        total = part if total is None else total + part
    return total


def spread_rows(spread_ref, rows):
    channels = rows.shape[-1]
    spread_ref[...] = jnp.zeros_like(spread_ref)
    for tap_a in range(3):
        spread_ref[pl.ds(64 * tap_a, 512), pl.ds(tap_a * channels, channels)] = rows


def add_taps(total_ref, spread_ref, slab_ref):
    total_ref[...] += jnp.dot(
        spread_ref[...].T, slab_ref[...], preferred_element_type=jnp.float32
    )


def write_taps(total_ref, grad_ref, scale):
    channels = grad_ref.shape[-1]
    for tap_a in range(3):
        for tap_bc in range(9):
            piece = total_ref[
                pl.ds(tap_a * channels, channels), pl.ds(tap_bc * channels, channels)
            ]
            grad_ref[9 * tap_a + tap_bc] = piece.T * scale


def sigmoid(values):
    return 1.0 / (1.0 + jnp.exp(-values))


def pack_kernel(own_ref, cot_ref, shell_ref):
    def step(block, carry):
        pack_shell(block, own_ref, shell_ref)
        pack_shell(block, cot_ref, shell_ref, SHELL)
        return carry

    lax.fori_loop(0, own_ref.shape[0], step, 0)


def first_kernel(
    place_ref, own_ref, table_ref, weight_ref, pre_ref, hidden_ref, shell_ref, pad_ref, slab_ref
):
    def step(block, carry):
        build_slab(block, own_ref, table_ref, place_ref, pad_ref, slab_ref)
        pre = conv_slab(slab_ref, weight_ref)
        pre_ref[block] = pre
        hidden = (pre / (1.0 + jnp.exp(-pre))).astype(jnp.bfloat16)
        hidden_ref[block] = hidden.reshape(hidden_ref.shape[1:])
        pack_shell(block, hidden_ref, shell_ref)
        return carry

    lax.fori_loop(0, own_ref.shape[0], step, 0)


def back_step(
    block, place_ref, own_ref, table_ref, cot_ref, weight_ref, pre_ref,
    pad_ref, slab_ref, spread_ref, total_ref,
):
    build_slab(block, cot_ref, table_ref, place_ref, pad_ref, slab_ref, SHELL)
    back = conv_slab(slab_ref, weight_ref)
    pre = pre_ref[block]
    sig = sigmoid(pre)
    delta = (back * (sig * (1.0 + pre * (1.0 - sig)))).astype(jnp.bfloat16)
    spread_rows(spread_ref, delta)
    build_slab(block, own_ref, table_ref, place_ref, pad_ref, slab_ref)
    add_taps(total_ref, spread_ref, slab_ref)


def back_kernel(scale, place_ref, own_ref, table_ref, cot_ref, weight_ref, pre_ref, grad_ref, *scratch):
    total_ref = scratch[-1]
    total_ref[...] = jnp.zeros_like(total_ref)

    def step(block, carry):
        back_step(
            block, place_ref, own_ref, table_ref, cot_ref, weight_ref, pre_ref, *scratch
        )
        return carry

    lax.fori_loop(0, own_ref.shape[0], step, 0)
    write_taps(total_ref, grad_ref, scale)


def back_ring_kernel(
    scale, devices, place_ref, own_ref, table_ref, cot_ref, weight_ref, pre_ref, payload_ref,
    grad_ref, hidden_table_ref, pad_ref, slab_ref, spread_ref, total_ref, *sems,
):
    begin, advance, finish = ring(devices, payload_ref, hidden_table_ref, *sems)
    begin()
    total_ref[...] = jnp.zeros_like(total_ref)
    count = own_ref.shape[0]

    def step(block, carry):
        back_step(
            block, place_ref, own_ref, table_ref, cot_ref, weight_ref, pre_ref,
            pad_ref, slab_ref, spread_ref, total_ref,
        )
        advance(block, False)
        return carry

    lax.fori_loop(0, count, step, 0)
    write_taps(total_ref, grad_ref, scale)
    for later in range(count, devices - 1):
        advance(later, later == devices - 2)
    finish()


def second_kernel(
    scale, place_ref, own_ref, table_ref, cot_ref, weight_ref,
    out_ref, grad_ref, pad_ref, slab_ref, spread_ref, total_ref,
):
    total_ref[...] = jnp.zeros_like(total_ref)

    def step(block, carry):
        build_slab(block, own_ref, table_ref, place_ref, pad_ref, slab_ref)
        out_ref[block] = conv_slab(slab_ref, weight_ref).astype(jnp.bfloat16)
        spread_rows(spread_ref, cot_ref[block].reshape(512, cot_ref.shape[-1]))
        add_taps(total_ref, spread_ref, slab_ref)
        return carry

    lax.fori_loop(0, own_ref.shape[0], step, 0)
    write_taps(total_ref, grad_ref, scale)


def ring(devices, payload_ref, table_ref, send_sem, recv_sem, own_sem):
    count = payload_ref.shape[0]
    half = count // 2
    cut = payload_ref.shape[1] // CUTS
    me = lax.axis_index("blocks")
    odd = me % 2
    pos = (1 - odd) * (me // 2) + odd * (devices - 1 - me // 2)
    pieces = [(part, way) for part in range(half * CUTS) for way in range(2)]

    def index_of(position):
        spot = (position + 2 * devices) % devices
        back = spot // (devices // 2)
        return (1 - back) * 2 * spot + back * (2 * (devices - 1 - spot) + 1)

    ends = (index_of(pos + 1), index_of(pos - 1))
    own = pltpu.make_async_copy(payload_ref, table_ref.at[pl.ds(me * count, count)], own_sem)

    def copy_at(step, part, way, first):
        owner = index_of(pos - (1 - 2 * way) * step)
        block = way * half + part // CUTS
        rows = pl.ds(part % CUTS * cut, cut)
        target = table_ref.at[owner * count + block, rows]
        return pltpu.make_async_remote_copy(
            src_ref=payload_ref.at[block, rows] if first else target,
            dst_ref=target,
            send_sem=send_sem.at[way, step, part],
            recv_sem=recv_sem.at[way, step, part],
            device_id={"blocks": ends[way]},
            device_id_type=pl.DeviceIdType.MESH,
        )

    def begin():
        barrier = pltpu.get_barrier_semaphore()
        for end in ends:
            pl.semaphore_signal(
                barrier, inc=1, device_id={"blocks": end}, device_id_type=pl.DeviceIdType.MESH
            )
        pl.semaphore_wait(barrier, 2)
        for part, way in pieces:
            copy_at(0, part, way, True).start()
        own.start()

    def advance(step, last):
        for part, way in pieces:
            copy_at(step, part, way, False).wait_recv()
            if not last:
                copy_at(step + 1, part, way, False).start()

    def finish():
        for step in range(devices - 1):
            for part, way in pieces:
                copy_at(step, part, way, step == 0).wait_send()
        own.wait()

    return begin, advance, finish


def ring_kernel(devices, payload_ref, table_ref, *sems):
    begin, advance, finish = ring(devices, payload_ref, table_ref, *sems)
    begin()
    for step in range(devices - 1):
        advance(step, step == devices - 2)
    finish()


def ring_sems(devices, count):
    sems = pltpu.SemaphoreType.DMA((2, devices - 1, count // 2 * CUTS))
    return [sems, sems, pltpu.SemaphoreType.DMA]


def ring_table(payload, devices):
    return jax.ShapeDtypeStruct((devices * payload.shape[0],) + payload.shape[1:], payload.dtype)


def bit_orders(block_bits, rep_bits):
    first = [("rep", 0)]
    rest = [("rep", k) for k in range(1, rep_bits)]
    low = [("blocks", k) for k in range(block_bits - 1)]
    last = [("blocks", block_bits - 1)]
    turning = rest + low
    turns = [turning[t % len(turning) :] + turning[: t % len(turning)] for t in range(3)]
    return [first + turn + last for turn in turns] * 2


def sum_kernel(orders, one_ref, two_ref, out_ref, held_ref, land_ref, send_sem, recv_sem):
    rows = out_ref.shape[0]
    levels = len(orders[0])
    unit, parts = 8 << levels, len(orders)
    cuts = [unit * (rows // unit * part // parts) for part in range(parts + 1)]
    shares = [cuts[part + 1] - cuts[part] for part in range(parts)]
    place = {axis: lax.axis_index(axis) for axis in ("blocks", "rep")}

    def bit_of(dim):
        axis, k = dim
        return place[axis] // 2**k % 2

    def partner(dim):
        axis, k = dim
        return {axis: place[axis] + (1 - 2 * bit_of(dim)) * 2**k}

    barrier = pltpu.get_barrier_semaphore()
    for dim in orders[0]:
        pl.semaphore_signal(
            barrier, inc=1, device_id=partner(dim), device_id_type=pl.DeviceIdType.MESH
        )
    pl.semaphore_wait(barrier, levels)
    held_ref[pl.ds(0, rows // 2), :] = one_ref[...]
    held_ref[pl.ds(rows // 2, rows // 2), :] = two_ref[...]

    def copy_to(part, step, dim, source, target):
        return pltpu.make_async_remote_copy(
            src_ref=source,
            dst_ref=target,
            send_sem=send_sem.at[part, step],
            recv_sem=recv_sem.at[part, step],
            device_id=partner(dim),
            device_id_type=pl.DeviceIdType.MESH,
        )

    starts = [[cuts[part]] for part in range(parts)]
    flying = [None] * len(orders)
    sent = []
    for step in range(levels + 1):
        for part, order in enumerate(orders):
            half = shares[part] >> (step + 1)
            if step:
                flying[part].wait_recv()
                size = shares[part] >> step
                mine = pl.ds(pl.multiple_of(starts[part][-1], 8), size)
                landed = pl.ds(cuts[part + 1] - 2 * size, size)
                summed = held_ref[mine, :] + land_ref[landed, :]
                kept_ref = held_ref if step < levels else out_ref
                kept_ref[mine, :] = summed
            if step < levels:
                bit = bit_of(order[step])
                start = starts[part][-1]
                away = pl.multiple_of(start + (1 - bit) * half, 8)
                copy = copy_to(
                    part, step, order[step],
                    held_ref.at[pl.ds(away, half)],
                    land_ref.at[pl.ds(cuts[part + 1] - 2 * half, half)],
                )
                copy.start()
                flying[part] = copy
                sent.append(copy)
                starts[part].append(start + bit * half)
    for step in reversed(range(levels)):
        for part, order in enumerate(orders):
            size = shares[part] >> (step + 1)
            if step < levels - 1:
                flying[part].wait_recv()
            mine = out_ref.at[pl.ds(pl.multiple_of(starts[part][step + 1], 8), size)]
            copy = copy_to(part, levels + step, order[step], mine, mine)
            copy.start()
            flying[part] = copy
            sent.append(copy)
    for copy in flying:
        copy.wait_recv()
    for copy in sent:
        copy.wait_send()


def sum_everywhere(one, two, block_devices, rep_devices, collective_id):
    block_bits, rep_bits = block_devices.bit_length() - 1, rep_devices.bit_length() - 1
    orders = bit_orders(block_bits, rep_bits)
    channels = one.shape[-1]
    rows = 2 * one.size // channels
    space = pl.BlockSpec(memory_space=pltpu.VMEM)
    sems = pltpu.SemaphoreType.DMA((len(orders), 2 * len(orders[0])))
    out = pl.pallas_call(
        functools.partial(sum_kernel, orders),
        out_shape=jax.ShapeDtypeStruct((rows, channels), one.dtype),
        in_specs=[space, space],
        out_specs=space,
        scratch_shapes=[pltpu.VMEM((rows, channels), one.dtype)] * 2 + [sems, sems],
        compiler_params=pltpu.CompilerParams(
            collective_id=collective_id, has_side_effects=True, vmem_limit_bytes=VMEM_LIMIT
        ),
    )(one.reshape(-1, channels), two.reshape(-1, channels))
    return out[: rows // 2].reshape(one.shape), out[rows // 2 :].reshape(two.shape)


def can_halve(count, rows):
    block_devices, rep_devices = count
    total = block_devices * rep_devices
    powers = total & (total - 1) == 0 and block_devices >= 2 and rep_devices >= 2
    return powers and rows % (8 * total) == 0 and rows >= 6 * 8 * total


def call(body, outs, scratch, flops, *operands, **params):
    space = pl.BlockSpec(memory_space=pltpu.VMEM)
    scalars = pl.BlockSpec(memory_space=pltpu.SMEM)
    specs = [scalars if x.dtype == jnp.int32 else space for x in operands]
    moved = sum(x.size * x.dtype.itemsize for x in operands)
    return pl.pallas_call(
        body,
        out_shape=outs,
        in_specs=specs,
        out_specs=[space] * len(outs),
        scratch_shapes=scratch,
        compiler_params=pltpu.CompilerParams(vmem_limit_bytes=VMEM_LIMIT, **params),
        cost_estimate=pl.CostEstimate(flops=flops, bytes_accessed=moved, transcendentals=0),
    )(*operands)


def local(features, weight_one, weight_two, cotangent, neighbours):
    block_count, channels = features.shape[1], features.shape[3]
    devices = lax.axis_size("blocks")
    reach = (block_count + 24) // block_count
    own = features[0].reshape(block_count, 8, 64, channels)
    cot = cotangent[0].reshape(block_count, 8, 64, channels)
    links = neighbours[0]
    whole = devices <= 2 * reach + 1
    if whole:
        placed = links
    else:
        gap = links // block_count - lax.axis_index("blocks")
        placed = jnp.where(links >= 0, (gap + reach) * block_count + links % block_count, -1)

    ringed = whole and devices % 2 == 0 and block_count % 2 == 0

    def collect(payload, collective_id):
        if ringed:
            (table,) = call(
                functools.partial(ring_kernel, devices),
                [ring_table(payload, devices)], ring_sems(devices, block_count), 0, payload,
                collective_id=collective_id, has_side_effects=True,
            )
            return table
        if whole:
            return lax.all_gather(payload, "blocks", axis=0, tiled=True)
        pieces = [
            payload if gap == 0 else from_behind(payload, "blocks", -gap)
            for gap in range(-reach, reach + 1)
        ]
        return jnp.concatenate(pieces, axis=0)

    def slabs(weights):
        return weights.reshape(3, 9 * channels, channels)

    flipped = jnp.transpose(weight_two[::-1], (0, 2, 1))
    voxels = lax.axis_size("rep") * devices * block_count * 512
    scale = 1.0 / math.sqrt(voxels)
    flops = 2 * block_count * 512 * 27 * channels * channels
    f32, bf16 = jnp.float32, jnp.bfloat16
    pad = pltpu.VMEM((3, 10, 80, channels), f32)
    slab = pltpu.VMEM((640, 9 * channels), bf16)
    spread = pltpu.VMEM((640, 3 * channels), bf16)
    total = pltpu.VMEM((3 * channels, 9 * channels), f32)
    rows = (block_count, 512, channels)
    grads = jax.ShapeDtypeStruct(weight_one.shape, f32)

    shell = jax.ShapeDtypeStruct((block_count, SHELL, channels), bf16)
    both = jax.ShapeDtypeStruct((block_count, 2 * SHELL, channels), bf16)

    (shells,) = call(pack_kernel, [both], [], 0, own, cot)
    table = collect(shells, 1)
    pre, hidden, hidden_shell = call(
        first_kernel,
        [jax.ShapeDtypeStruct(rows, f32), jax.ShapeDtypeStruct(own.shape, bf16), shell],
        [pad, slab], flops,
        placed, own, table, slabs(weight_one),
    )
    back_operands = (placed, own, table, cot, slabs(flipped), pre)
    back_scratch = [pad, slab, spread, total]
    if ringed and block_count < devices - 1:
        grad_one, hidden_table = call(
            functools.partial(back_ring_kernel, scale, devices),
            [grads, ring_table(hidden_shell, devices)],
            back_scratch + ring_sems(devices, block_count), 2 * flops,
            *back_operands, hidden_shell,
            collective_id=2, has_side_effects=True,
        )
    else:
        hidden_table = collect(hidden_shell, 2)
        (grad_one,) = call(
            functools.partial(back_kernel, scale), [grads], back_scratch, 2 * flops, *back_operands
        )
    out, grad_two = call(
        functools.partial(second_kernel, scale),
        [jax.ShapeDtypeStruct(rows, bf16), grads], [pad, slab, spread, total], 2 * flops,
        placed, hidden, hidden_table, cot, slabs(weight_two),
    )
    counts = (devices, lax.axis_size("rep"))
    if can_halve(counts, 2 * grad_one.size // channels):
        grad_one, grad_two = sum_everywhere(grad_one, grad_two, *counts, 3)
    else:
        grad_one, grad_two = lax.psum((grad_one, grad_two), ("blocks", "rep"))
    return out.reshape(features.shape), grad_one, grad_two


def solution(mesh):
    in_specs = (
        P("rep", "blocks", None, None),
        P(),
        P(),
        P("rep", "blocks", None, None),
        P("rep", "blocks", None),
    )
    out_specs = (P("rep", "blocks", None, None), P(), P())
    return jax.shard_map(local, mesh=mesh, in_specs=in_specs, out_specs=out_specs, check_vma=False)
```

```python
import functools
import math

import jax
import jax.numpy as jnp
from jax import lax
from jax.experimental import pallas as pl
from jax.experimental.pallas import tpu as pltpu
from jax.sharding import PartitionSpec as P

VMEM_LIMIT = 56 * 1024 * 1024
SHELL = 320
CUTS = 2


def offset_index(step_x, step_y, step_z):
    place = 9 * (step_x + 1) + 3 * (step_y + 1) + (step_z + 1)
    return place if place < 13 else place - 1


def from_behind(block, axis, distance):
    devices = range(lax.axis_size(axis))
    route = [(i - distance, i) for i in devices if i - distance in devices]
    return lax.ppermute(block, axis, route)


def lines_of(rows):
    return rows.astype(jnp.float32).reshape(-1, 8, rows.shape[-1])


def plane_start(plane):
    return {0: 0, 7: 64}.get(plane, 128 + 32 * (plane - 1))


def pack_shell(block, own_ref, shell_ref):
    channels = own_ref.shape[-1]
    for plane in (0, 7):
        shell_ref[block, pl.ds(plane_start(plane), 64), :] = own_ref[block, plane]
    for plane in range(1, 7):
        lines = lines_of(own_ref[block, plane])
        cell = lax.broadcasted_iota(jnp.int32, (1, 8, channels), 1)
        ends = []
        for group in (0, 4):
            packed = pltpu.roll(lines[group : group + 1], 1, 1)
            for turn in range(1, 4):
                line = pltpu.roll(lines[group + turn : group + turn + 1], 2 * turn + 1, 1)
                packed = jnp.where(cell >= 2 * turn, line, packed)
            ends.append(packed)
        packed = jnp.concatenate([lines[0:1], lines[7:8]] + ends, axis=0)
        packed = packed.reshape(32, channels).astype(jnp.bfloat16)
        shell_ref[block, pl.ds(plane_start(plane), 32), :] = packed


def build_slab(block, own_ref, table_ref, place_ref, pad_ref, slab_ref):
    channels = own_ref.shape[-1]

    def source(step_x, step_y, step_z, plane):
        if (step_x, step_y, step_z) == (0, 0, 0):
            return lines_of(own_ref[block, plane])
        where = place_ref[block, offset_index(step_x, step_y, step_z)]
        near, start = jnp.maximum(where, 0), plane_start(plane)
        if plane in (0, 7):
            if step_y == 0:
                got = lines_of(table_ref[near, pl.ds(start, 64), :])
            elif step_y == 1:
                got = lines_of(table_ref[near, pl.ds(start, 16), :])[0:1]
            else:
                got = lines_of(table_ref[near, pl.ds(start + 48, 16), :])[1:2]
        elif step_y == 0:
            ends = lines_of(table_ref[near, pl.ds(start + 16, 16), :])
            got = jnp.concatenate(
                [
                    pltpu.roll(ends[j // 4 : j // 4 + 1], 7 - 2 * (j % 4), 1)
                    for j in range(8)
                ],
                axis=0,
            )
        else:
            got = lines_of(table_ref[near, pl.ds(start, 16), :])
            got = got[0:1] if step_y == 1 else got[1:2]
        return jnp.where(where >= 0, got, 0.0)

    def put(ii, first_line, step_x, step_y, plane):
        mid, low, high = (source(step_x, step_y, step_z, plane) for step_z in (0, -1, 1))
        cell = lax.broadcasted_iota(jnp.int32, mid.shape, 1)
        count = mid.shape[0]
        shifted = (
            pltpu.roll(jnp.where(cell == 7, low, mid), 1, 1),
            mid,
            pltpu.roll(jnp.where(cell == 0, high, mid), 7, 1),
        )
        for tap_c in range(3):
            pad_ref[tap_c, ii, pl.ds(8 * first_line, 8 * count), :] = shifted[tap_c].reshape(
                8 * count, channels
            )

    for ii in range(10):
        step_x = -1 if ii == 0 else (1 if ii == 9 else 0)
        plane = 7 if ii == 0 else (0 if ii == 9 else ii - 1)
        put(ii, 0, step_x, -1, plane)
        put(ii, 1, step_x, 0, plane)
        put(ii, 9, step_x, 1, plane)
    for tap_b in range(3):
        for tap_c in range(3):
            column = (3 * tap_b + tap_c) * channels
            slab_ref[:, pl.ds(column, channels)] = (
                pad_ref[tap_c, :, pl.ds(8 * tap_b, 64), :]
                .reshape(640, channels)
                .astype(jnp.bfloat16)
            )


def conv_slab(slab_ref, weight_ref):
    total = None
    for tap_a in range(3):
        part = jnp.dot(
            slab_ref[pl.ds(64 * tap_a, 512), :],
            weight_ref[tap_a],
            preferred_element_type=jnp.float32,
        )
        total = part if total is None else total + part
    return total


def spread_rows(spread_ref, rows):
    channels = rows.shape[-1]
    spread_ref[...] = jnp.zeros_like(spread_ref)
    for tap_a in range(3):
        spread_ref[pl.ds(64 * tap_a, 512), pl.ds(tap_a * channels, channels)] = rows


def add_taps(total_ref, spread_ref, slab_ref):
    total_ref[...] += jnp.dot(
        spread_ref[...].T, slab_ref[...], preferred_element_type=jnp.float32
    )


def write_taps(total_ref, grad_ref, scale):
    channels = grad_ref.shape[-1]
    for tap_a in range(3):
        for tap_bc in range(9):
            piece = total_ref[
                pl.ds(tap_a * channels, channels), pl.ds(tap_bc * channels, channels)
            ]
            grad_ref[9 * tap_a + tap_bc] = piece.T * scale


def sigmoid(values):
    return 1.0 / (1.0 + jnp.exp(-values))


def pack_all(field_ref, shell_ref):
    def step(block, carry):
        pack_shell(block, field_ref, shell_ref)
        return carry

    lax.fori_loop(0, field_ref.shape[0], step, 0)


def flip_taps(weight_ref, flipped_ref):
    taps = weight_ref.shape[0]
    for tap in range(taps):
        flipped_ref[tap] = weight_ref[taps - 1 - tap].T


def pack_kernel(own_ref, cot_ref, weight_ref, shell_ref, cot_shell_ref, flipped_ref):
    pack_all(own_ref, shell_ref)
    pack_all(cot_ref, cot_shell_ref)
    flip_taps(weight_ref, flipped_ref)


def pack_ring_kernel(
    devices, own_ref, cot_ref, weight_ref, table_ref, cot_shell_ref, flipped_ref, shell_ref, *sems
):
    pack_all(own_ref, shell_ref)
    begin, advance, finish = ring(devices, shell_ref, table_ref, *sems)
    begin()
    pack_all(cot_ref, cot_shell_ref)
    flip_taps(weight_ref, flipped_ref)
    for step in range(devices - 1):
        advance(step, step == devices - 2)
    finish()


def first_step(
    block, place_ref, own_ref, table_ref, weight_ref, pre_ref, hidden_ref, shell_ref,
    pad_ref, slab_ref,
):
    build_slab(block, own_ref, table_ref, place_ref, pad_ref, slab_ref)
    pre = conv_slab(slab_ref, weight_ref)
    pre_ref[block] = pre
    hidden = (pre / (1.0 + jnp.exp(-pre))).astype(jnp.bfloat16)
    hidden_ref[block] = hidden.reshape(hidden_ref.shape[1:])
    pack_shell(block, hidden_ref, shell_ref)


def first_kernel(*refs):
    def step(block, carry):
        first_step(block, *refs)
        return carry

    lax.fori_loop(0, refs[1].shape[0], step, 0)


def first_ring_kernel(
    devices, place_ref, own_ref, table_ref, weight_ref, payload_ref,
    pre_ref, hidden_ref, shell_ref, cot_table_ref, pad_ref, slab_ref, *sems,
):
    begin, advance, finish = ring(devices, payload_ref, cot_table_ref, *sems)
    begin()
    count = own_ref.shape[0]

    def step(block, carry):
        first_step(
            block, place_ref, own_ref, table_ref, weight_ref, pre_ref, hidden_ref, shell_ref,
            pad_ref, slab_ref,
        )
        advance(block, False)
        return carry

    lax.fori_loop(0, count, step, 0)
    for later in range(count, devices - 1):
        advance(later, later == devices - 2)
    finish()


def back_step(
    block, place_ref, own_ref, table_ref, cot_ref, cot_table_ref, weight_ref, pre_ref,
    pad_ref, slab_ref, spread_ref, total_ref,
):
    build_slab(block, cot_ref, cot_table_ref, place_ref, pad_ref, slab_ref)
    back = conv_slab(slab_ref, weight_ref)
    pre = pre_ref[block]
    sig = sigmoid(pre)
    delta = (back * (sig * (1.0 + pre * (1.0 - sig)))).astype(jnp.bfloat16)
    spread_rows(spread_ref, delta)
    build_slab(block, own_ref, table_ref, place_ref, pad_ref, slab_ref)
    add_taps(total_ref, spread_ref, slab_ref)


def back_kernel(
    scale, place_ref, own_ref, table_ref, cot_ref, cot_table_ref, weight_ref, pre_ref, grad_ref,
    *scratch,
):
    total_ref = scratch[-1]
    total_ref[...] = jnp.zeros_like(total_ref)

    def step(block, carry):
        back_step(
            block, place_ref, own_ref, table_ref, cot_ref, cot_table_ref, weight_ref, pre_ref,
            *scratch,
        )
        return carry

    lax.fori_loop(0, own_ref.shape[0], step, 0)
    write_taps(total_ref, grad_ref, scale)


def back_ring_kernel(
    scale, devices, place_ref, own_ref, table_ref, cot_ref, cot_table_ref, weight_ref, pre_ref,
    payload_ref,
    grad_ref, hidden_table_ref, pad_ref, slab_ref, spread_ref, total_ref, *sems,
):
    begin, advance, finish = ring(devices, payload_ref, hidden_table_ref, *sems)
    begin()
    total_ref[...] = jnp.zeros_like(total_ref)
    count = own_ref.shape[0]

    def step(block, carry):
        back_step(
            block, place_ref, own_ref, table_ref, cot_ref, cot_table_ref, weight_ref, pre_ref,
            pad_ref, slab_ref, spread_ref, total_ref,
        )
        advance(block, False)
        return carry

    lax.fori_loop(0, count, step, 0)
    write_taps(total_ref, grad_ref, scale)
    for later in range(count, devices - 1):
        advance(later, later == devices - 2)
    finish()


def second_kernel(
    scale, place_ref, own_ref, table_ref, cot_ref, weight_ref,
    out_ref, grad_ref, pad_ref, slab_ref, spread_ref, total_ref,
):
    total_ref[...] = jnp.zeros_like(total_ref)

    def step(block, carry):
        build_slab(block, own_ref, table_ref, place_ref, pad_ref, slab_ref)
        out_ref[block] = conv_slab(slab_ref, weight_ref).astype(jnp.bfloat16)
        spread_rows(spread_ref, cot_ref[block].reshape(512, cot_ref.shape[-1]))
        add_taps(total_ref, spread_ref, slab_ref)
        return carry

    lax.fori_loop(0, own_ref.shape[0], step, 0)
    write_taps(total_ref, grad_ref, scale)


def ring(devices, payload_ref, table_ref, send_sem, recv_sem, own_sem):
    count = payload_ref.shape[0]
    half = count // 2
    cut = payload_ref.shape[1] // CUTS
    me = lax.axis_index("blocks")
    odd = me % 2
    pos = (1 - odd) * (me // 2) + odd * (devices - 1 - me // 2)
    pieces = [(part, way) for part in range(half * CUTS) for way in range(2)]

    def index_of(position):
        spot = (position + 2 * devices) % devices
        back = spot // (devices // 2)
        return (1 - back) * 2 * spot + back * (2 * (devices - 1 - spot) + 1)

    ends = (index_of(pos + 1), index_of(pos - 1))
    own = pltpu.make_async_copy(payload_ref, table_ref.at[pl.ds(me * count, count)], own_sem)

    def copy_at(step, part, way, first):
        owner = index_of(pos - (1 - 2 * way) * step)
        block = way * half + part // CUTS
        rows = pl.ds(part % CUTS * cut, cut)
        target = table_ref.at[owner * count + block, rows]
        return pltpu.make_async_remote_copy(
            src_ref=payload_ref.at[block, rows] if first else target,
            dst_ref=target,
            send_sem=send_sem.at[way, step, part],
            recv_sem=recv_sem.at[way, step, part],
            device_id={"blocks": ends[way]},
            device_id_type=pl.DeviceIdType.MESH,
        )

    def begin():
        barrier = pltpu.get_barrier_semaphore()
        for end in ends:
            pl.semaphore_signal(
                barrier, inc=1, device_id={"blocks": end}, device_id_type=pl.DeviceIdType.MESH
            )
        pl.semaphore_wait(barrier, 2)
        for part, way in pieces:
            copy_at(0, part, way, True).start()
        own.start()

    def advance(step, last):
        for part, way in pieces:
            copy_at(step, part, way, False).wait_recv()
            if not last:
                copy_at(step + 1, part, way, False).start()

    def finish():
        for step in range(devices - 1):
            for part, way in pieces:
                copy_at(step, part, way, step == 0).wait_send()
        own.wait()

    return begin, advance, finish


def ring_sems(devices, count):
    sems = pltpu.SemaphoreType.DMA((2, devices - 1, count // 2 * CUTS))
    return [sems, sems, pltpu.SemaphoreType.DMA]


def ring_table(payload, devices):
    return jax.ShapeDtypeStruct((devices * payload.shape[0],) + payload.shape[1:], payload.dtype)


def bit_orders(block_bits, rep_bits):
    first = [("rep", 0)]
    rest = [("rep", k) for k in range(1, rep_bits)]
    low = [("blocks", k) for k in range(block_bits - 1)]
    last = [("blocks", block_bits - 1)]
    turning = rest + low
    turns = [turning[t % len(turning) :] + turning[: t % len(turning)] for t in range(3)]
    return [first + turn + last for turn in turns] * 2


def sum_kernel(orders, one_ref, two_ref, out_ref, held_ref, land_ref, send_sem, recv_sem):
    rows = out_ref.shape[0]
    levels = len(orders[0])
    unit, parts = 8 << levels, len(orders)
    cuts = [unit * (rows // unit * part // parts) for part in range(parts + 1)]
    shares = [cuts[part + 1] - cuts[part] for part in range(parts)]
    place = {axis: lax.axis_index(axis) for axis in ("blocks", "rep")}

    def bit_of(dim):
        axis, k = dim
        return place[axis] // 2**k % 2

    def partner(dim):
        axis, k = dim
        return {axis: place[axis] + (1 - 2 * bit_of(dim)) * 2**k}

    barrier = pltpu.get_barrier_semaphore()
    for dim in orders[0]:
        pl.semaphore_signal(
            barrier, inc=1, device_id=partner(dim), device_id_type=pl.DeviceIdType.MESH
        )
    pl.semaphore_wait(barrier, levels)
    held_ref[pl.ds(0, rows // 2), :] = one_ref[...]
    held_ref[pl.ds(rows // 2, rows // 2), :] = two_ref[...]

    def copy_to(part, step, dim, source, target):
        return pltpu.make_async_remote_copy(
            src_ref=source,
            dst_ref=target,
            send_sem=send_sem.at[part, step],
            recv_sem=recv_sem.at[part, step],
            device_id=partner(dim),
            device_id_type=pl.DeviceIdType.MESH,
        )

    starts = [[cuts[part]] for part in range(parts)]
    flying = [None] * len(orders)
    sent = []
    for step in range(levels + 1):
        for part, order in enumerate(orders):
            half = shares[part] >> (step + 1)
            if step:
                flying[part].wait_recv()
                size = shares[part] >> step
                mine = pl.ds(pl.multiple_of(starts[part][-1], 8), size)
                landed = pl.ds(cuts[part + 1] - 2 * size, size)
                summed = held_ref[mine, :] + land_ref[landed, :]
                kept_ref = held_ref if step < levels else out_ref
                kept_ref[mine, :] = summed
            if step < levels:
                bit = bit_of(order[step])
                start = starts[part][-1]
                away = pl.multiple_of(start + (1 - bit) * half, 8)
                copy = copy_to(
                    part, step, order[step],
                    held_ref.at[pl.ds(away, half)],
                    land_ref.at[pl.ds(cuts[part + 1] - 2 * half, half)],
                )
                copy.start()
                flying[part] = copy
                sent.append(copy)
                starts[part].append(start + bit * half)
    for step in reversed(range(levels)):
        for part, order in enumerate(orders):
            size = shares[part] >> (step + 1)
            if step < levels - 1:
                flying[part].wait_recv()
            mine = out_ref.at[pl.ds(pl.multiple_of(starts[part][step + 1], 8), size)]
            copy = copy_to(part, levels + step, order[step], mine, mine)
            copy.start()
            flying[part] = copy
            sent.append(copy)
    for copy in flying:
        copy.wait_recv()
    for copy in sent:
        copy.wait_send()


def sum_everywhere(one, two, block_devices, rep_devices, collective_id):
    block_bits, rep_bits = block_devices.bit_length() - 1, rep_devices.bit_length() - 1
    orders = bit_orders(block_bits, rep_bits)
    channels = one.shape[-1]
    rows = 2 * one.size // channels
    space = pl.BlockSpec(memory_space=pltpu.VMEM)
    sems = pltpu.SemaphoreType.DMA((len(orders), 2 * len(orders[0])))
    out = pl.pallas_call(
        functools.partial(sum_kernel, orders),
        out_shape=jax.ShapeDtypeStruct((rows, channels), one.dtype),
        in_specs=[space, space],
        out_specs=space,
        scratch_shapes=[pltpu.VMEM((rows, channels), one.dtype)] * 2 + [sems, sems],
        compiler_params=pltpu.CompilerParams(
            collective_id=collective_id, has_side_effects=True, vmem_limit_bytes=VMEM_LIMIT
        ),
    )(one.reshape(-1, channels), two.reshape(-1, channels))
    return out[: rows // 2].reshape(one.shape), out[rows // 2 :].reshape(two.shape)


def can_halve(count, rows):
    block_devices, rep_devices = count
    total = block_devices * rep_devices
    powers = total & (total - 1) == 0 and block_devices >= 2 and rep_devices >= 2
    return powers and rows % (8 * total) == 0 and rows >= 6 * 8 * total


def call(body, outs, scratch, flops, *operands, **params):
    space = pl.BlockSpec(memory_space=pltpu.VMEM)
    scalars = pl.BlockSpec(memory_space=pltpu.SMEM)
    specs = [scalars if x.dtype == jnp.int32 else space for x in operands]
    moved = sum(x.size * x.dtype.itemsize for x in operands)
    return pl.pallas_call(
        body,
        out_shape=outs,
        in_specs=specs,
        out_specs=[space] * len(outs),
        scratch_shapes=scratch,
        compiler_params=pltpu.CompilerParams(vmem_limit_bytes=VMEM_LIMIT, **params),
        cost_estimate=pl.CostEstimate(flops=flops, bytes_accessed=moved, transcendentals=0),
    )(*operands)


def local(features, weight_one, weight_two, cotangent, neighbours):
    block_count, channels = features.shape[1], features.shape[3]
    devices = lax.axis_size("blocks")
    reach = (block_count + 24) // block_count
    own = features[0].reshape(block_count, 8, 64, channels)
    cot = cotangent[0].reshape(block_count, 8, 64, channels)
    links = neighbours[0]
    whole = devices <= 2 * reach + 1
    if whole:
        placed = links
    else:
        gap = links // block_count - lax.axis_index("blocks")
        placed = jnp.where(links >= 0, (gap + reach) * block_count + links % block_count, -1)

    ringed = whole and devices % 2 == 0 and block_count % 2 == 0 and block_count < devices - 1

    def collect(payload):
        if whole:
            return lax.all_gather(payload, "blocks", axis=0, tiled=True)
        pieces = [
            payload if gap == 0 else from_behind(payload, "blocks", -gap)
            for gap in range(-reach, reach + 1)
        ]
        return jnp.concatenate(pieces, axis=0)

    def slabs(weights):
        return weights.reshape(3, 9 * channels, channels)

    voxels = lax.axis_size("rep") * devices * block_count * 512
    scale = 1.0 / math.sqrt(voxels)
    flops = 2 * block_count * 512 * 27 * channels * channels
    f32, bf16 = jnp.float32, jnp.bfloat16
    pad = pltpu.VMEM((3, 10, 80, channels), f32)
    slab = pltpu.VMEM((640, 9 * channels), bf16)
    spread = pltpu.VMEM((640, 3 * channels), bf16)
    total = pltpu.VMEM((3 * channels, 9 * channels), f32)
    rows = (block_count, 512, channels)
    grads = jax.ShapeDtypeStruct(weight_one.shape, f32)

    shell = jax.ShapeDtypeStruct((block_count, SHELL, channels), bf16)
    flipped_taps = jax.ShapeDtypeStruct(weight_two.shape, bf16)
    pre_and_hidden = [
        jax.ShapeDtypeStruct(rows, f32), jax.ShapeDtypeStruct(own.shape, bf16), shell
    ]
    back_scratch = [pad, slab, spread, total]
    if ringed:
        gathered, sems = ring_table(shell, devices), ring_sems(devices, block_count)
        table, cot_shell, flipped = call(
            functools.partial(pack_ring_kernel, devices), [gathered, shell, flipped_taps],
            [pltpu.VMEM(shell.shape, bf16)] + sems, 0, own, cot, weight_two,
            collective_id=1, has_side_effects=True,
        )
        pre, hidden, hidden_shell, cot_table = call(
            functools.partial(first_ring_kernel, devices), pre_and_hidden + [gathered],
            [pad, slab] + sems, flops,
            placed, own, table, slabs(weight_one), cot_shell,
            collective_id=2, has_side_effects=True,
        )
        grad_one, hidden_table = call(
            functools.partial(back_ring_kernel, scale, devices), [grads, gathered],
            back_scratch + sems, 2 * flops,
            placed, own, table, cot, cot_table, slabs(flipped), pre, hidden_shell,
            collective_id=3, has_side_effects=True,
        )
    else:
        own_shell, cot_shell, flipped = call(
            pack_kernel, [shell, shell, flipped_taps], [], 0, own, cot, weight_two
        )
        table, cot_table = collect(own_shell), collect(cot_shell)
        pre, hidden, hidden_shell = call(
            first_kernel, pre_and_hidden, [pad, slab], flops,
            placed, own, table, slabs(weight_one),
        )
        hidden_table = collect(hidden_shell)
        (grad_one,) = call(
            functools.partial(back_kernel, scale), [grads], back_scratch, 2 * flops,
            placed, own, table, cot, cot_table, slabs(flipped), pre,
        )
    out, grad_two = call(
        functools.partial(second_kernel, scale),
        [jax.ShapeDtypeStruct(rows, bf16), grads], [pad, slab, spread, total], 2 * flops,
        placed, hidden, hidden_table, cot, slabs(weight_two),
    )
    counts = (devices, lax.axis_size("rep"))
    if can_halve(counts, 2 * grad_one.size // channels):
        grad_one, grad_two = sum_everywhere(grad_one, grad_two, *counts, 4)
    else:
        grad_one, grad_two = lax.psum((grad_one, grad_two), ("blocks", "rep"))
    return out.reshape(features.shape), grad_one, grad_two


def solution(mesh):
    in_specs = (
        P("rep", "blocks", None, None),
        P(),
        P(),
        P("rep", "blocks", None, None),
        P("rep", "blocks", None),
    )
    out_specs = (P("rep", "blocks", None, None), P(), P())
    return jax.shard_map(local, mesh=mesh, in_specs=in_specs, out_specs=out_specs, check_vma=False)
```

```python
import functools
import math

import jax
import jax.numpy as jnp
from jax import lax
from jax.experimental import pallas as pl
from jax.experimental.pallas import tpu as pltpu
from jax.sharding import PartitionSpec as P

VMEM_LIMIT = 56 * 1024 * 1024
SHELL = 320
CUTS = 2


def offset_index(step_x, step_y, step_z):
    place = 9 * (step_x + 1) + 3 * (step_y + 1) + (step_z + 1)
    return place if place < 13 else place - 1


def from_behind(block, axis, distance):
    devices = range(lax.axis_size(axis))
    route = [(i - distance, i) for i in devices if i - distance in devices]
    return lax.ppermute(block, axis, route)


def lines_of(rows):
    return rows.astype(jnp.float32).reshape(-1, 8, rows.shape[-1])


def plane_start(plane):
    return {0: 0, 7: 64}.get(plane, 128 + 32 * (plane - 1))


def pack_shell(block, own_ref, shell_ref):
    channels = own_ref.shape[-1]
    for plane in (0, 7):
        shell_ref[block, pl.ds(plane_start(plane), 64), :] = own_ref[block, plane]
    for plane in range(1, 7):
        lines = lines_of(own_ref[block, plane])
        cell = lax.broadcasted_iota(jnp.int32, (1, 8, channels), 1)
        ends = []
        for group in (0, 4):
            packed = pltpu.roll(lines[group : group + 1], 1, 1)
            for turn in range(1, 4):
                line = pltpu.roll(lines[group + turn : group + turn + 1], 2 * turn + 1, 1)
                packed = jnp.where(cell >= 2 * turn, line, packed)
            ends.append(packed)
        packed = jnp.concatenate([lines[0:1], lines[7:8]] + ends, axis=0)
        packed = packed.reshape(32, channels).astype(jnp.bfloat16)
        shell_ref[block, pl.ds(plane_start(plane), 32), :] = packed


def build_slab(block, own_ref, table_ref, place_ref, pad_ref, slab_ref):
    channels = own_ref.shape[-1]

    def source(step_x, step_y, step_z, plane):
        if (step_x, step_y, step_z) == (0, 0, 0):
            return lines_of(own_ref[block, plane])
        where = place_ref[block, offset_index(step_x, step_y, step_z)]
        near, start = jnp.maximum(where, 0), plane_start(plane)
        if plane in (0, 7):
            if step_y == 0:
                got = lines_of(table_ref[near, pl.ds(start, 64), :])
            elif step_y == 1:
                got = lines_of(table_ref[near, pl.ds(start, 16), :])[0:1]
            else:
                got = lines_of(table_ref[near, pl.ds(start + 48, 16), :])[1:2]
        elif step_y == 0:
            ends = lines_of(table_ref[near, pl.ds(start + 16, 16), :])
            got = jnp.concatenate(
                [
                    pltpu.roll(ends[j // 4 : j // 4 + 1], 7 - 2 * (j % 4), 1)
                    for j in range(8)
                ],
                axis=0,
            )
        else:
            got = lines_of(table_ref[near, pl.ds(start, 16), :])
            got = got[0:1] if step_y == 1 else got[1:2]
        return jnp.where(where >= 0, got, 0.0)

    def put(ii, first_line, step_x, step_y, plane):
        mid, low, high = (source(step_x, step_y, step_z, plane) for step_z in (0, -1, 1))
        cell = lax.broadcasted_iota(jnp.int32, mid.shape, 1)
        count = mid.shape[0]
        shifted = (
            pltpu.roll(jnp.where(cell == 7, low, mid), 1, 1),
            mid,
            pltpu.roll(jnp.where(cell == 0, high, mid), 7, 1),
        )
        for tap_c in range(3):
            pad_ref[tap_c, ii, pl.ds(8 * first_line, 8 * count), :] = shifted[tap_c].reshape(
                8 * count, channels
            )

    for ii in range(10):
        step_x = -1 if ii == 0 else (1 if ii == 9 else 0)
        plane = 7 if ii == 0 else (0 if ii == 9 else ii - 1)
        put(ii, 0, step_x, -1, plane)
        put(ii, 1, step_x, 0, plane)
        put(ii, 9, step_x, 1, plane)
    for tap_b in range(3):
        for tap_c in range(3):
            column = (3 * tap_b + tap_c) * channels
            slab_ref[:, pl.ds(column, channels)] = (
                pad_ref[tap_c, :, pl.ds(8 * tap_b, 64), :]
                .reshape(640, channels)
                .astype(jnp.bfloat16)
            )


def conv_slab(slab_ref, weight_ref):
    total = None
    for tap_a in range(3):
        part = jnp.dot(
            slab_ref[pl.ds(64 * tap_a, 512), :],
            weight_ref[tap_a],
            preferred_element_type=jnp.float32,
        )
        total = part if total is None else total + part
    return total


def spread_rows(spread_ref, rows):
    channels = rows.shape[-1]
    spread_ref[...] = jnp.zeros_like(spread_ref)
    for tap_a in range(3):
        spread_ref[pl.ds(64 * tap_a, 512), pl.ds(tap_a * channels, channels)] = rows


def add_taps(total_ref, spread_ref, slab_ref):
    total_ref[...] += jnp.dot(
        spread_ref[...].T, slab_ref[...], preferred_element_type=jnp.float32
    )


def write_taps(total_ref, grad_ref, scale):
    channels = grad_ref.shape[-1]
    for tap_a in range(3):
        for tap_bc in range(9):
            piece = total_ref[
                pl.ds(tap_a * channels, channels), pl.ds(tap_bc * channels, channels)
            ]
            grad_ref[9 * tap_a + tap_bc] = piece.T * scale


def sigmoid(values):
    return 1.0 / (1.0 + jnp.exp(-values))


def pack_all(field_ref, shell_ref):
    def step(block, carry):
        pack_shell(block, field_ref, shell_ref)
        return carry

    lax.fori_loop(0, field_ref.shape[0], step, 0)


def flip_taps(weight_ref, flipped_ref):
    taps = weight_ref.shape[0]
    for tap in range(taps):
        flipped_ref[tap] = weight_ref[taps - 1 - tap].T


def pack_kernel(own_ref, cot_ref, weight_ref, shell_ref, cot_shell_ref, flipped_ref):
    pack_all(own_ref, shell_ref)
    pack_all(cot_ref, cot_shell_ref)
    flip_taps(weight_ref, flipped_ref)


def pack_ring_kernel(
    devices, own_ref, cot_ref, weight_ref, table_ref, cot_shell_ref, flipped_ref, shell_ref, *sems
):
    pack_all(own_ref, shell_ref)
    begin, advance, finish = ring(devices, shell_ref, table_ref, *sems)
    begin()
    pack_all(cot_ref, cot_shell_ref)
    flip_taps(weight_ref, flipped_ref)
    for step in range(devices - 1):
        advance(step, step == devices - 2)
    finish()


def first_step(
    block, place_ref, own_ref, table_ref, weight_ref, pre_ref, hidden_ref, shell_ref,
    pad_ref, slab_ref,
):
    build_slab(block, own_ref, table_ref, place_ref, pad_ref, slab_ref)
    pre = conv_slab(slab_ref, weight_ref)
    pre_ref[block] = pre
    hidden = (pre / (1.0 + jnp.exp(-pre))).astype(jnp.bfloat16)
    hidden_ref[block] = hidden.reshape(hidden_ref.shape[1:])
    pack_shell(block, hidden_ref, shell_ref)


def first_kernel(*refs):
    def step(block, carry):
        first_step(block, *refs)
        return carry

    lax.fori_loop(0, refs[1].shape[0], step, 0)


def first_ring_kernel(
    devices, place_ref, own_ref, table_ref, weight_ref, payload_ref,
    pre_ref, hidden_ref, shell_ref, cot_table_ref, pad_ref, slab_ref, *sems,
):
    begin, advance, finish = ring(devices, payload_ref, cot_table_ref, *sems)
    begin()
    count = own_ref.shape[0]

    def step(block, carry):
        first_step(
            block, place_ref, own_ref, table_ref, weight_ref, pre_ref, hidden_ref, shell_ref,
            pad_ref, slab_ref,
        )
        advance(block, False)
        return carry

    lax.fori_loop(0, count, step, 0)
    for later in range(count, devices - 1):
        advance(later, later == devices - 2)
    finish()


def back_step(
    block, place_ref, own_ref, table_ref, cot_ref, cot_table_ref, weight_ref, pre_ref,
    pad_ref, slab_ref, spread_ref, total_ref,
):
    build_slab(block, cot_ref, cot_table_ref, place_ref, pad_ref, slab_ref)
    back = conv_slab(slab_ref, weight_ref)
    pre = pre_ref[block]
    sig = sigmoid(pre)
    delta = (back * (sig * (1.0 + pre * (1.0 - sig)))).astype(jnp.bfloat16)
    spread_rows(spread_ref, delta)
    build_slab(block, own_ref, table_ref, place_ref, pad_ref, slab_ref)
    add_taps(total_ref, spread_ref, slab_ref)


def back_kernel(
    scale, place_ref, own_ref, table_ref, cot_ref, cot_table_ref, weight_ref, pre_ref, grad_ref,
    *scratch,
):
    total_ref = scratch[-1]
    total_ref[...] = jnp.zeros_like(total_ref)

    def step(block, carry):
        back_step(
            block, place_ref, own_ref, table_ref, cot_ref, cot_table_ref, weight_ref, pre_ref,
            *scratch,
        )
        return carry

    lax.fori_loop(0, own_ref.shape[0], step, 0)
    write_taps(total_ref, grad_ref, scale)


def back_ring_kernel(
    scale, devices, place_ref, own_ref, table_ref, cot_ref, cot_table_ref, weight_ref, pre_ref,
    payload_ref,
    grad_ref, hidden_table_ref, pad_ref, slab_ref, spread_ref, total_ref, *sems,
):
    begin, advance, finish = ring(devices, payload_ref, hidden_table_ref, *sems)
    begin()
    total_ref[...] = jnp.zeros_like(total_ref)
    count = own_ref.shape[0]

    def step(block, carry):
        back_step(
            block, place_ref, own_ref, table_ref, cot_ref, cot_table_ref, weight_ref, pre_ref,
            pad_ref, slab_ref, spread_ref, total_ref,
        )
        advance(block, False)
        return carry

    lax.fori_loop(0, count, step, 0)
    write_taps(total_ref, grad_ref, scale)
    for later in range(count, devices - 1):
        advance(later, later == devices - 2)
    finish()


def second_kernel(
    scale, place_ref, own_ref, table_ref, cot_ref, weight_ref,
    out_ref, grad_ref, pad_ref, slab_ref, spread_ref, total_ref,
):
    total_ref[...] = jnp.zeros_like(total_ref)

    def step(block, carry):
        build_slab(block, own_ref, table_ref, place_ref, pad_ref, slab_ref)
        out_ref[block] = conv_slab(slab_ref, weight_ref).astype(jnp.bfloat16)
        spread_rows(spread_ref, cot_ref[block].reshape(512, cot_ref.shape[-1]))
        add_taps(total_ref, spread_ref, slab_ref)
        return carry

    lax.fori_loop(0, own_ref.shape[0], step, 0)
    write_taps(total_ref, grad_ref, scale)


def ring(devices, payload_ref, table_ref, send_sem, recv_sem, own_sem):
    count = payload_ref.shape[0]
    half = count // 2
    cut = payload_ref.shape[1] // CUTS
    me = lax.axis_index("blocks")
    odd = me % 2
    pos = (1 - odd) * (me // 2) + odd * (devices - 1 - me // 2)
    pieces = [(part, way) for part in range(half * CUTS) for way in range(2)]

    def index_of(position):
        spot = (position + 2 * devices) % devices
        back = spot // (devices // 2)
        return (1 - back) * 2 * spot + back * (2 * (devices - 1 - spot) + 1)

    ends = (index_of(pos + 1), index_of(pos - 1))
    own = pltpu.make_async_copy(payload_ref, table_ref.at[pl.ds(me * count, count)], own_sem)

    def copy_at(step, part, way, first):
        owner = index_of(pos - (1 - 2 * way) * step)
        block = way * half + part // CUTS
        rows = pl.ds(part % CUTS * cut, cut)
        target = table_ref.at[owner * count + block, rows]
        return pltpu.make_async_remote_copy(
            src_ref=payload_ref.at[block, rows] if first else target,
            dst_ref=target,
            send_sem=send_sem.at[way, step, part],
            recv_sem=recv_sem.at[way, step, part],
            device_id={"blocks": ends[way]},
            device_id_type=pl.DeviceIdType.MESH,
        )

    def begin():
        barrier = pltpu.get_barrier_semaphore()
        for end in ends:
            pl.semaphore_signal(
                barrier, inc=1, device_id={"blocks": end}, device_id_type=pl.DeviceIdType.MESH
            )
        pl.semaphore_wait(barrier, 2)
        for part, way in pieces:
            copy_at(0, part, way, True).start()
        own.start()

    def advance(step, last):
        for part, way in pieces:
            copy_at(step, part, way, False).wait_recv()
            if not last:
                copy_at(step + 1, part, way, False).start()

    def finish():
        for step in range(devices - 1):
            for part, way in pieces:
                copy_at(step, part, way, step == 0).wait_send()
        own.wait()

    return begin, advance, finish


def ring_sems(devices, count):
    sems = pltpu.SemaphoreType.DMA((2, devices - 1, count // 2 * CUTS))
    return [sems, sems, pltpu.SemaphoreType.DMA]


def ring_table(payload, devices):
    return jax.ShapeDtypeStruct((devices * payload.shape[0],) + payload.shape[1:], payload.dtype)


def bit_orders(block_bits, rep_bits):
    first = [("rep", 0)]
    rest = [("rep", k) for k in range(1, rep_bits)]
    low = [("blocks", k) for k in range(block_bits - 1)]
    last = [("blocks", block_bits - 1)]
    turning = rest + low
    turns = [turning[t % len(turning) :] + turning[: t % len(turning)] for t in range(3)]
    return [first + turn + last for turn in turns] * 2


def sum_kernel(orders, one_ref, two_ref, out_ref, held_ref, land_ref, send_sem, recv_sem):
    rows = out_ref.shape[0]
    levels = len(orders[0])
    unit, parts = 8 << levels, len(orders)
    cuts = [unit * (rows // unit * part // parts) for part in range(parts + 1)]
    shares = [cuts[part + 1] - cuts[part] for part in range(parts)]
    place = {axis: lax.axis_index(axis) for axis in ("blocks", "rep")}

    def bit_of(dim):
        axis, k = dim
        return place[axis] // 2**k % 2

    def partner(dim):
        axis, k = dim
        return {axis: place[axis] + (1 - 2 * bit_of(dim)) * 2**k}

    barrier = pltpu.get_barrier_semaphore()
    for dim in orders[0]:
        pl.semaphore_signal(
            barrier, inc=1, device_id=partner(dim), device_id_type=pl.DeviceIdType.MESH
        )
    pl.semaphore_wait(barrier, levels)

    def load(low, high):
        for source_ref, base in ((one_ref, 0), (two_ref, rows // 2)):
            first, end = max(low, base), min(high, base + rows // 2)
            if first < end:
                held_ref[pl.ds(first, end - first), :] = source_ref[
                    pl.ds(first - base, end - first), :
                ]

    def copy_to(part, step, dim, source, target):
        return pltpu.make_async_remote_copy(
            src_ref=source,
            dst_ref=target,
            send_sem=send_sem.at[part, step],
            recv_sem=recv_sem.at[part, step],
            device_id=partner(dim),
            device_id_type=pl.DeviceIdType.MESH,
        )

    starts = [[cuts[part]] for part in range(parts)]
    flying = [None] * len(orders)
    sent = []
    for step in range(levels + 1):
        for part, order in enumerate(orders):
            half = shares[part] >> (step + 1)
            if step == 0:
                load(cuts[part], cuts[part + 1])
            else:
                flying[part].wait_recv()
                size = shares[part] >> step
                mine = pl.ds(pl.multiple_of(starts[part][-1], 8), size)
                landed = pl.ds(cuts[part + 1] - 2 * size, size)
                summed = held_ref[mine, :] + land_ref[landed, :]
                kept_ref = held_ref if step < levels else out_ref
                kept_ref[mine, :] = summed
            if step < levels:
                bit = bit_of(order[step])
                start = starts[part][-1]
                away = pl.multiple_of(start + (1 - bit) * half, 8)
                copy = copy_to(
                    part, step, order[step],
                    held_ref.at[pl.ds(away, half)],
                    land_ref.at[pl.ds(cuts[part + 1] - 2 * half, half)],
                )
                copy.start()
                flying[part] = copy
                sent.append(copy)
                starts[part].append(start + bit * half)
    for step in reversed(range(levels)):
        for part, order in enumerate(orders):
            size = shares[part] >> (step + 1)
            if step < levels - 1:
                flying[part].wait_recv()
            mine = out_ref.at[pl.ds(pl.multiple_of(starts[part][step + 1], 8), size)]
            copy = copy_to(part, levels + step, order[step], mine, mine)
            copy.start()
            flying[part] = copy
            sent.append(copy)
    for copy in flying:
        copy.wait_recv()
    for copy in sent:
        copy.wait_send()


def sum_everywhere(one, two, block_devices, rep_devices, collective_id):
    block_bits, rep_bits = block_devices.bit_length() - 1, rep_devices.bit_length() - 1
    orders = bit_orders(block_bits, rep_bits)
    channels = one.shape[-1]
    rows = 2 * one.size // channels
    space = pl.BlockSpec(memory_space=pltpu.VMEM)
    sems = pltpu.SemaphoreType.DMA((len(orders), 2 * len(orders[0])))
    out = pl.pallas_call(
        functools.partial(sum_kernel, orders),
        out_shape=jax.ShapeDtypeStruct((rows, channels), one.dtype),
        in_specs=[space, space],
        out_specs=space,
        scratch_shapes=[pltpu.VMEM((rows, channels), one.dtype)] * 2 + [sems, sems],
        compiler_params=pltpu.CompilerParams(
            collective_id=collective_id, has_side_effects=True, vmem_limit_bytes=VMEM_LIMIT
        ),
    )(one.reshape(-1, channels), two.reshape(-1, channels))
    return out[: rows // 2].reshape(one.shape), out[rows // 2 :].reshape(two.shape)


def can_halve(count, rows):
    block_devices, rep_devices = count
    total = block_devices * rep_devices
    powers = total & (total - 1) == 0 and block_devices >= 2 and rep_devices >= 2
    return powers and rows % (8 * total) == 0 and rows >= 6 * 8 * total


def call(body, outs, scratch, flops, *operands, **params):
    space = pl.BlockSpec(memory_space=pltpu.VMEM)
    scalars = pl.BlockSpec(memory_space=pltpu.SMEM)
    specs = [scalars if x.dtype == jnp.int32 else space for x in operands]
    moved = sum(x.size * x.dtype.itemsize for x in operands)
    return pl.pallas_call(
        body,
        out_shape=outs,
        in_specs=specs,
        out_specs=[space] * len(outs),
        scratch_shapes=scratch,
        compiler_params=pltpu.CompilerParams(vmem_limit_bytes=VMEM_LIMIT, **params),
        cost_estimate=pl.CostEstimate(flops=flops, bytes_accessed=moved, transcendentals=0),
    )(*operands)


def local(features, weight_one, weight_two, cotangent, neighbours):
    block_count, channels = features.shape[1], features.shape[3]
    devices = lax.axis_size("blocks")
    reach = (block_count + 24) // block_count
    own = features[0].reshape(block_count, 8, 64, channels)
    cot = cotangent[0].reshape(block_count, 8, 64, channels)
    links = neighbours[0]
    whole = devices <= 2 * reach + 1
    if whole:
        placed = links
    else:
        gap = links // block_count - lax.axis_index("blocks")
        placed = jnp.where(links >= 0, (gap + reach) * block_count + links % block_count, -1)

    ringed = whole and devices % 2 == 0 and block_count % 2 == 0 and block_count < devices - 1

    def collect(payload):
        if whole:
            return lax.all_gather(payload, "blocks", axis=0, tiled=True)
        pieces = [
            payload if gap == 0 else from_behind(payload, "blocks", -gap)
            for gap in range(-reach, reach + 1)
        ]
        return jnp.concatenate(pieces, axis=0)

    def slabs(weights):
        return weights.reshape(3, 9 * channels, channels)

    voxels = lax.axis_size("rep") * devices * block_count * 512
    scale = 1.0 / math.sqrt(voxels)
    flops = 2 * block_count * 512 * 27 * channels * channels
    f32, bf16 = jnp.float32, jnp.bfloat16
    pad = pltpu.VMEM((3, 10, 80, channels), f32)
    slab = pltpu.VMEM((640, 9 * channels), bf16)
    spread = pltpu.VMEM((640, 3 * channels), bf16)
    total = pltpu.VMEM((3 * channels, 9 * channels), f32)
    rows = (block_count, 512, channels)
    grads = jax.ShapeDtypeStruct(weight_one.shape, f32)

    shell = jax.ShapeDtypeStruct((block_count, SHELL, channels), bf16)
    flipped_taps = jax.ShapeDtypeStruct(weight_two.shape, bf16)
    pre_and_hidden = [
        jax.ShapeDtypeStruct(rows, f32), jax.ShapeDtypeStruct(own.shape, bf16), shell
    ]
    back_scratch = [pad, slab, spread, total]
    if ringed:
        gathered, sems = ring_table(shell, devices), ring_sems(devices, block_count)
        table, cot_shell, flipped = call(
            functools.partial(pack_ring_kernel, devices), [gathered, shell, flipped_taps],
            [pltpu.VMEM(shell.shape, bf16)] + sems, 0, own, cot, weight_two,
            collective_id=1, has_side_effects=True,
        )
        pre, hidden, hidden_shell, cot_table = call(
            functools.partial(first_ring_kernel, devices), pre_and_hidden + [gathered],
            [pad, slab] + sems, flops,
            placed, own, table, slabs(weight_one), cot_shell,
            collective_id=2, has_side_effects=True,
        )
        grad_one, hidden_table = call(
            functools.partial(back_ring_kernel, scale, devices), [grads, gathered],
            back_scratch + sems, 2 * flops,
            placed, own, table, cot, cot_table, slabs(flipped), pre, hidden_shell,
            collective_id=3, has_side_effects=True,
        )
    else:
        own_shell, cot_shell, flipped = call(
            pack_kernel, [shell, shell, flipped_taps], [], 0, own, cot, weight_two
        )
        table, cot_table = collect(own_shell), collect(cot_shell)
        pre, hidden, hidden_shell = call(
            first_kernel, pre_and_hidden, [pad, slab], flops,
            placed, own, table, slabs(weight_one),
        )
        hidden_table = collect(hidden_shell)
        (grad_one,) = call(
            functools.partial(back_kernel, scale), [grads], back_scratch, 2 * flops,
            placed, own, table, cot, cot_table, slabs(flipped), pre,
        )
    out, grad_two = call(
        functools.partial(second_kernel, scale),
        [jax.ShapeDtypeStruct(rows, bf16), grads], [pad, slab, spread, total], 2 * flops,
        placed, hidden, hidden_table, cot, slabs(weight_two),
    )
    counts = (devices, lax.axis_size("rep"))
    if can_halve(counts, 2 * grad_one.size // channels):
        grad_one, grad_two = sum_everywhere(grad_one, grad_two, *counts, 4)
    else:
        grad_one, grad_two = lax.psum((grad_one, grad_two), ("blocks", "rep"))
    return out.reshape(features.shape), grad_one, grad_two


def solution(mesh):
    in_specs = (
        P("rep", "blocks", None, None),
        P(),
        P(),
        P("rep", "blocks", None, None),
        P("rep", "blocks", None),
    )
    out_specs = (P("rep", "blocks", None, None), P(), P())
    return jax.shard_map(local, mesh=mesh, in_specs=in_specs, out_specs=out_specs, check_vma=False)
```
